128 devices in a mesh: blk: 16 (over x, z_lo, core), smp: 8 (over y, z_hi).
Axes of the slice: x: 4, y: 4, z: 4 (z_hi: 2, z_lo: 2; z = z_hi * 2 + z_lo), core: 2. Of those that a mesh axis runs over, the one named last changes fastest.
Arguments:
- scaled_genotype_counts: bfloat16 [16384, 8192], P('smp', 'blk'), may hold values from -6 to 6
- adjusted_trait_scores: bfloat16 [16384, 8], P('smp'), may hold values from -6 to 6
- subset_membership: int32 [16384], P('smp'), may hold values from 0 to 4, as said below
- regularizer_lambdas: float32 [2], replicated, may hold values from 0.01 to 0.1
- unseen_subset_guesses: bfloat16 [8, 2048, 8, 32], P('smp', 'blk'), may hold values from -6 to 6
Outputs:
- oof: bfloat16 [16384, 8, 32], P('smp', None, 'blk')
- cross: float32 [8, 32, 64], P(None, 'blk', 'smp')
The draws below stay inside these ranges and needn't reach their ends.
Inputs may be any that keep to these rules, and one draw needn't show every extreme that they name: `subset_membership`: every fold holds some samples.
All inputs are finite; a program needn't handle non-finite values.
Results may differ from the reference program's by a relative error of at most 0.0047.
Values may be sent and summed in bfloat16 or wider, within the bound.
A program may use at most 128 MiB of HBM per device.

```python
import math
import jax
import jax.numpy as jnp
from jax import lax

BLOCK = 512
PHENOTYPIC_MEASURES = 8
FOLDS = 5
SHRINK_STRENGTH = 2
PER_DEVICE_CASES = 2048
SAMPLES = 16384
VARIANTS = 8192
PRIOR_ESTIMATES = 32


def shared_factor(key):
    anchor = jax.random.fold_in(key, 9001)
    ancestry = jax.random.normal(jax.random.fold_in(anchor, 1), (SAMPLES,), jnp.float32)
    trait_load = jax.random.uniform(jax.random.fold_in(anchor, 2), (PHENOTYPIC_MEASURES,), jnp.float32, 0.15, 0.35)
    return (ancestry, trait_load)


def draw_scaled_genotype_counts(key, part):
    nblocks = VARIANTS // BLOCK
    cohorts = SAMPLES // PER_DEVICE_CASES
    ancestry, trait_load = shared_factor(key)
    anchor = jax.random.fold_in(key, 4711)
    low_gap, high_gap = (math.log(0.02), math.log(0.5))
    low_scale, high_scale = (math.log(0.4), math.log(2.5))
    mixing = 0.1
    spacing = jnp.exp(jax.random.uniform(jax.random.fold_in(anchor, 1), (cohorts, nblocks), jnp.float32, low_gap, high_gap))
    retain = 1.0 - spacing
    renewal = jnp.sqrt(1.0 - retain * retain)
    row_cohort = jnp.arange(SAMPLES, dtype=jnp.int32) // PER_DEVICE_CASES
    retain_rows = retain[row_cohort]
    renewal_rows = renewal[row_cohort]
    noise_key = jax.random.fold_in(anchor, 2)

    def advance(carry, position):
        fresh = jax.random.normal(jax.random.fold_in(noise_key, position), (SAMPLES, nblocks), jnp.float32)
        value = jnp.where(position == 0, fresh, retain_rows * carry + renewal_rows * fresh)
        return (value, value)
    _, trajectory = lax.scan(advance, jnp.zeros((SAMPLES, nblocks), jnp.float32), jnp.arange(BLOCK, dtype=jnp.int32))
    chains = jnp.transpose(trajectory, (1, 2, 0))
    shuffles = jax.vmap(lambda subkey: jax.random.permutation(subkey, BLOCK))(jax.random.split(jax.random.fold_in(anchor, 3), nblocks))
    chains = jax.vmap(lambda block_values, columns: block_values[:, columns], in_axes=(1, 0), out_axes=1)(chains, shuffles)
    chains = chains.reshape(SAMPLES, VARIANTS)
    loading = jax.random.normal(jax.random.fold_in(anchor, 4), (VARIANTS,), jnp.float32)
    blended = math.sqrt(1.0 - mixing) * chains + math.sqrt(mixing) * ancestry[:, None] * loading[None, :]
    column_scale = jnp.exp(jax.random.uniform(jax.random.fold_in(anchor, 5), (cohorts, VARIANTS), jnp.float32, low_scale, high_scale))
    column_scale = column_scale / jnp.sqrt(jnp.mean(column_scale * column_scale, axis=0, keepdims=True))
    scaled = blended.reshape(cohorts, PER_DEVICE_CASES, VARIANTS) * column_scale[:, None, :]
    return jnp.clip(scaled.reshape(SAMPLES, VARIANTS), -6.0, 6.0).astype(jnp.bfloat16)


def draw_adjusted_trait_scores(key, part):
    ancestry, trait_load = shared_factor(key)
    noise_key = jax.random.fold_in(key, 5813)
    noise = jax.random.normal(noise_key, (SAMPLES, PHENOTYPIC_MEASURES), jnp.float32)
    shared_part = trait_load
    value = shared_part[None, :] * ancestry[:, None] + jnp.sqrt(1.0 - shared_part * shared_part)[None, :] * noise
    return jnp.clip(value, -6.0, 6.0).astype(jnp.bfloat16)


def draw_subset_membership(key, part):
    anchor = jax.random.fold_in(key, 3307)
    reach = SAMPLES // (4 * FOLDS)
    jitter = jax.random.randint(jax.random.fold_in(anchor, 1), (FOLDS - 1,), -reach, reach + 1, dtype=jnp.int32)
    bounds = jnp.arange(1, FOLDS, dtype=jnp.int32) * SAMPLES // FOLDS + jitter
    position = jnp.arange(SAMPLES, dtype=jnp.int32)
    contiguous = jnp.sum((position[:, None] >= bounds[None, :]).astype(jnp.int32), axis=1)
    stray = jax.random.randint(jax.random.fold_in(anchor, 2), (SAMPLES,), 0, 8, dtype=jnp.int32) == 0
    elsewhere = jax.random.randint(jax.random.fold_in(anchor, 3), (SAMPLES,), 0, FOLDS, dtype=jnp.int32)
    return jnp.where(stray, elsewhere, contiguous).astype(jnp.int32)


def draw_unseen_subset_guesses(key, part):
    ancestry, trait_load = shared_factor(key)
    anchor = jax.random.fold_in(key, 6151)
    feature_load = jax.random.uniform(jax.random.fold_in(anchor, 1), (PRIOR_ESTIMATES,), jnp.float32, 0.5, 1.5)
    noise_key = jax.random.fold_in(anchor, 2)
    noise = jax.random.normal(noise_key, (SAMPLES, PHENOTYPIC_MEASURES, PRIOR_ESTIMATES), jnp.float32)
    strength = 4.0
    value = strength * trait_load[None, :, None] * feature_load[None, None, :] * ancestry[:, None, None] + noise
    value = jnp.clip(value, -6.0, 6.0)
    cohorts = SAMPLES // PER_DEVICE_CASES
    return value.reshape(cohorts, PER_DEVICE_CASES, PHENOTYPIC_MEASURES, PRIOR_ESTIMATES).astype(jnp.bfloat16)


def setup_inputs(seed: int = 0) -> dict:
    keys = jax.random.split(jax.random.key(seed), 6)
    scaled_genotype_counts = draw_scaled_genotype_counts(jax.random.fold_in(keys[5], 71), 0)
    adjusted_trait_scores = draw_adjusted_trait_scores(jax.random.fold_in(keys[5], 71), 0)
    subset_membership = draw_subset_membership(jax.random.fold_in(keys[5], 71), 0)
    regularizer_lambdas = jnp.clip(jnp.exp(jax.random.uniform(keys[3], (SHRINK_STRENGTH,), jnp.float32, math.log(0.01), math.log(0.1))), 0.01, 0.1)
    unseen_subset_guesses = draw_unseen_subset_guesses(jax.random.fold_in(keys[5], 71), 0)
    return dict(scaled_genotype_counts=scaled_genotype_counts, adjusted_trait_scores=adjusted_trait_scores, subset_membership=subset_membership, regularizer_lambdas=regularizer_lambdas, unseen_subset_guesses=unseen_subset_guesses)


def train_locus_group(locus_group_span, adjusted_trait_scores, partition_indicator, regularizer_lambdas, person_entries):
    masked_values = locus_group_span.astype(jnp.float32)[:, None, :] * partition_indicator.astype(jnp.float32)[:, :, None]
    inner_covariance_stack = jnp.einsum('rpe,ro->peo', masked_values, locus_group_span.astype(jnp.float32), precision=lax.Precision.HIGHEST)
    pairwise_interaction_features = jnp.einsum('jdx,jr->dxr', masked_values, adjusted_trait_scores.astype(jnp.float32), precision=lax.Precision.HIGHEST)
    normal_equation_stack = lax.optimization_barrier(jnp.sum(inner_covariance_stack, axis=0))[None] - inner_covariance_stack
    equation_targets = lax.optimization_barrier(jnp.sum(pairwise_interaction_features, axis=0))[None] - pairwise_interaction_features
    unit_diagonal = jnp.eye(BLOCK, dtype=jnp.float32)
    solved = []
    for position_number in range(SHRINK_STRENGTH):
        regressor_array = normal_equation_stack + regularizer_lambdas[position_number] * person_entries * unit_diagonal
        factor = jnp.linalg.cholesky(regressor_array)
        solved.append(jax.vmap(lambda c, b: jax.scipy.linalg.cho_solve((c, True), b))(factor, equation_targets))
    weight_array = jnp.stack(solved, axis=-1)
    coeffs_half = jnp.transpose(weight_array, (1, 0, 2, 3)).astype(jnp.bfloat16)
    fitted = jnp.dot(locus_group_span.astype(jnp.float32), coeffs_half.reshape(BLOCK, -1).astype(jnp.float32), preferred_element_type=jnp.float32)
    fitted = fitted.reshape(locus_group_span.shape[0], FOLDS, PHENOTYPIC_MEASURES, SHRINK_STRENGTH)
    chosen = lax.optimization_barrier(jnp.sum(fitted * partition_indicator.astype(jnp.float32)[:, :, None, None], axis=1))
    return (chosen * math.sqrt(person_entries / BLOCK)).astype(jnp.bfloat16)

def reference(scaled_genotype_counts, adjusted_trait_scores, subset_membership, regularizer_lambdas, unseen_subset_guesses):
    person_entries = scaled_genotype_counts.shape[0]
    nblocks = scaled_genotype_counts.shape[1] // BLOCK
    partition_indicator = (subset_membership[:, None] == jnp.arange(FOLDS, dtype=jnp.int32)[None, :]).astype(jnp.bfloat16)

    def one_block(position_number):
        locus_group_span = lax.dynamic_slice_in_dim(scaled_genotype_counts, position_number * BLOCK, BLOCK, 1)
        return train_locus_group(locus_group_span, adjusted_trait_scores, partition_indicator, regularizer_lambdas, person_entries)
    fitted = lax.map(one_block, jnp.arange(nblocks, dtype=jnp.int32))
    oof = jnp.transpose(fitted, (1, 2, 0, 3)).reshape(person_entries, PHENOTYPIC_MEASURES, nblocks * SHRINK_STRENGTH)
    preceding = unseen_subset_guesses.reshape(person_entries, PHENOTYPIC_MEASURES, unseen_subset_guesses.shape[-1])
    joined = jnp.concatenate([preceding, oof], axis=2)
    cross = jnp.einsum('stf,stc->tfc', oof.astype(jnp.float32), joined.astype(jnp.float32), precision=lax.Precision.HIGHEST) / person_entries
    return (oof, cross)
```

```python
import math

import jax
import jax.numpy as jnp
from jax import lax
from jax.experimental import pallas as pl
from jax.experimental.pallas import tpu as pltpu
from jax.sharding import PartitionSpec as P

HI = lax.Precision.HIGHEST
NB = 4
BLK = [(p, q) for p in range(NB) for q in range(p, NB)]
IDX = {pq: i for i, pq in enumerate(BLK)}


def lanes(x, m):
    return jnp.broadcast_to(x[:, m:m + 1], x.shape)


def subl(x, m):
    return jnp.broadcast_to(x[m:m + 1, :], x.shape)


def sweep_step(groups):
    a0 = groups[0]
    lane = lax.broadcasted_iota(jnp.int32, (8, 128), 1)
    sub = lax.broadcasted_iota(jnp.int32, (8, 128), 0)
    cols = [lanes(a0, m) for m in range(8)]
    s = {(i, m): subl(cols[m], i) for m in range(8) for i in range(m, 8)}
    z = [jnp.where(lane < 8, jnp.where(lane == m, -1.0, 0.0), subl(a0, m)) for m in range(8)]
    d, l = [None] * 8, {}
    for m in range(8):
        d[m] = 1.0 / s[m, m]
        for i in range(m + 1, 8):
            l[i, m] = s[i, m] * d[m]
        for j in range(m + 1, 8):
            for i in range(j, 8):
                s[i, j] = s[i, j] - l[i, m] * s[j, m]
        for i in range(m + 1, 8):
            z[i] = z[i] - l[i, m] * z[m]
    q = [z[m] * d[m] for m in range(8)]
    for m in range(7, -1, -1):
        for i in range(m):
            q[i] = q[i] - l[m, i] * q[m]
    out = []
    for g in range(1, 16):
        a = groups[g]
        new = jnp.where(lane < 8, 0.0, a)
        for m in range(8):
            new = new - lanes(a, m) * q[m]
        out.append(pltpu.roll(new, 120, 1))
    new = q[0]
    for m in range(1, 8):
        new = jnp.where(sub == m, q[m], new)
    out.append(pltpu.roll(new, 120, 1))
    return out


def inverse(mats):
    def body(_, carry):
        return tuple(tuple(sweep_step(list(c))) for c in carry)
    init = tuple(tuple(m[8 * g:8 * g + 8, :] for g in range(16)) for m in mats)
    out = lax.fori_loop(0, 16, body, init)
    return [-jnp.concatenate(list(c), axis=0) for c in out]


def dot(a, b, ca=1, cb=0):
    return lax.dot_general(a, b, (((ca,), (cb,)), ((), ())), precision=HI, preferred_element_type=jnp.float32)


def solve_kernel(lam_ref, a_ref, b_ref, out_ref, s_ref, t_ref, y_ref, w_ref):
    n = 16384.0
    row = lax.broadcasted_iota(jnp.int32, (128, 128), 0)
    col = lax.broadcasted_iota(jnp.int32, (128, 128), 1)
    for j in range(2):
        shift = lam_ref[j] * n
        for p in range(NB):
            for q in range(p, NB):
                v = a_ref[IDX[p, q]]
                if p == q:
                    v = v + jnp.where(row == col, shift, 0.0)
                s_ref[j, p, :, 128 * q:128 * q + 128] = v
        y_ref[j] = b_ref[...]
    for p in range(NB):
        lo, hi = 128 * p, 128 * p + 128
        ws = inverse([s_ref[j, p, :, lo:hi] for j in range(2)])
        for j in range(2):
            w = ws[j]
            y = dot(y_ref[j, :, lo:hi], w)
            y_ref[j, :, lo:hi] = y
            if p + 1 < NB:
                right = s_ref[j, p, :, hi:]
                t = dot(w, right)
                t_ref[j, p, :, hi:] = t
                y_ref[j, :, hi:] = y_ref[j, :, hi:] - dot(y, right)
                for q in range(p + 1, NB):
                    k = 128 * q
                    s_ref[j, q, :, k:] = s_ref[j, q, :, k:] - dot(s_ref[j, p, :, k:k + 128], t_ref[j, p, :, k:], 0, 0)
    for j in range(2):
        for p in range(NB - 2, -1, -1):
            lo, hi = 128 * p, 128 * p + 128
            y_ref[j, :, lo:hi] = y_ref[j, :, lo:hi] - dot(y_ref[j, :, hi:], t_ref[j, p, :, hi:], 1, 1)
    for t in range(8):
        for j in range(2):
            out_ref[2 * t + j:2 * t + j + 1, :] = y_ref[j, t:t + 1, :]


def solve(lam, a, b):
    return pl.pallas_call(
        solve_kernel,
        out_shape=jax.ShapeDtypeStruct((16, 512), jnp.float32),
        in_specs=[pl.BlockSpec(memory_space=pltpu.SMEM), pl.BlockSpec(memory_space=pltpu.VMEM), pl.BlockSpec(memory_space=pltpu.VMEM)],
        out_specs=pl.BlockSpec(memory_space=pltpu.VMEM),
        scratch_shapes=[pltpu.VMEM((2, 4, 128, 512), jnp.float32), pltpu.VMEM((2, 4, 128, 512), jnp.float32), pltpu.VMEM((2, 8, 512), jnp.float32), pltpu.VMEM((2, 128, 128), jnp.float32)],
        compiler_params=pltpu.CompilerParams(vmem_limit_bytes=40 << 20),
    )(lam, a, b)


FOLDS = 5
BLOCK = 512
TRAITS = 8


def local(x, y, fold, lam, old):
    rows = x.shape[0]
    person_entries = rows * lax.axis_size("smp")
    scale = 1.0 / person_entries
    ind = (fold[:, None] == jnp.arange(FOLDS, dtype=jnp.int32)[None, :]).astype(jnp.bfloat16)
    masked = x[:, None, :] * ind[:, :, None]
    gram = jnp.einsum("rpe,ro->peo", masked, x, preferred_element_type=jnp.float32)
    xy = jnp.einsum("jdx,jr->drx", masked, y, preferred_element_type=jnp.float32)
    gram, xy = lax.psum((gram, xy), "smp")
    mine = jnp.minimum(lax.axis_index("smp"), FOLDS - 1)
    a = jnp.sum(gram, axis=0) - lax.dynamic_index_in_dim(gram, mine, 0, keepdims=False)
    b = jnp.sum(xy, axis=0) - lax.dynamic_index_in_dim(xy, mine, 0, keepdims=False)
    blocks = jnp.stack([a[128 * p:128 * p + 128, 128 * q:128 * q + 128] for p, q in BLK])
    beta = solve(lam, blocks, b).astype(jnp.bfloat16)
    betas = lax.all_gather(beta, "smp", axis=0)[:FOLDS].reshape(FOLDS * 16, BLOCK)
    fitted = lax.dot_general(betas, x, (((1,), (1,)), ((), ())), preferred_element_type=jnp.float32)
    fitted = fitted.reshape(FOLDS, 16, rows)
    chosen = jnp.zeros((16, rows), jnp.float32)
    for k in range(FOLDS):
        chosen = jnp.where(fold[None, :] == k, fitted[k], chosen)
    oof = (chosen * math.sqrt(person_entries / BLOCK)).astype(jnp.bfloat16).reshape(TRAITS, 2, rows)
    everyone = lax.all_gather(oof, "blk", axis=1, tiled=True)
    new_part = jnp.einsum("tfs,tcs->tfc", oof, everyone, preferred_element_type=jnp.float32)
    before = lax.all_gather(old, "blk", axis=1, tiled=True)[0]
    old_part = jnp.einsum("tfs,stc->tfc", oof, before, preferred_element_type=jnp.float32)
    partial_value = jnp.concatenate([old_part, new_part], axis=2) * scale
    cross = lax.psum_scatter(partial_value, "smp", scatter_dimension=2, tiled=True)
    return jnp.transpose(oof, (2, 0, 1)), cross


def solution(mesh):
    return jax.shard_map(
        local,
        mesh=mesh,
        in_specs=(P("smp", "blk"), P("smp", None), P("smp"), P(), P("smp", "blk", None, None)),
        out_specs=(P("smp", None, "blk"), P(None, "blk", "smp")),
        check_vma=False,
    )
```

```python
import math

import jax
import jax.numpy as jnp
from jax import lax
from jax.experimental import pallas as pl
from jax.experimental.pallas import tpu as pltpu
from jax.sharding import PartitionSpec as P

HI = lax.Precision.HIGHEST
NB = 4
BLK = [(p, q) for p in range(NB) for q in range(p, NB)]
IDX = {pq: i for i, pq in enumerate(BLK)}


def lanes(x, m):
    return jnp.broadcast_to(x[:, m:m + 1], x.shape)


def subl(x, m):
    return jnp.broadcast_to(x[m:m + 1, :], x.shape)


def sweep_step(groups):
    a0 = groups[0]
    lane = lax.broadcasted_iota(jnp.int32, (8, 128), 1)
    sub = lax.broadcasted_iota(jnp.int32, (8, 128), 0)
    cols = [lanes(a0, m) for m in range(8)]
    s = {(i, m): subl(cols[m], i) for m in range(8) for i in range(m, 8)}
    z = [jnp.where(lane < 8, jnp.where(lane == m, -1.0, 0.0), subl(a0, m)) for m in range(8)]
    d, l = [None] * 8, {}
    for m in range(8):
        d[m] = 1.0 / s[m, m]
        for i in range(m + 1, 8):
            l[i, m] = s[i, m] * d[m]
        for j in range(m + 1, 8):
            for i in range(j, 8):
                s[i, j] = s[i, j] - l[i, m] * s[j, m]
        for i in range(m + 1, 8):
            z[i] = z[i] - l[i, m] * z[m]
    q = [z[m] * d[m] for m in range(8)]
    for m in range(7, -1, -1):
        for i in range(m):
            q[i] = q[i] - l[m, i] * q[m]
    out = []
    for g in range(1, 16):
        a = groups[g]
        new = jnp.where(lane < 8, 0.0, a)
        for m in range(8):
            new = new - lanes(a, m) * q[m]
        out.append(pltpu.roll(new, 120, 1))
    new = q[0]
    for m in range(1, 8):
        new = jnp.where(sub == m, q[m], new)
    out.append(pltpu.roll(new, 120, 1))
    return out


def inverse(mats):
    def body(_, carry):
        return tuple(tuple(sweep_step(list(c))) for c in carry)
    init = tuple(tuple(m[8 * g:8 * g + 8, :] for g in range(16)) for m in mats)
    out = lax.fori_loop(0, 16, body, init)
    return [-jnp.concatenate(list(c), axis=0) for c in out]


def dot(a, b, ca=1, cb=0):
    return lax.dot_general(a, b, (((ca,), (cb,)), ((), ())), precision=HI, preferred_element_type=jnp.float32)


def solve_kernel(lam_ref, a_ref, out_ref, s_ref, t_ref, y_ref, x_ref):
    n = 16384.0
    row = lax.broadcasted_iota(jnp.int32, (128, 128), 0)
    col = lax.broadcasted_iota(jnp.int32, (128, 128), 1)
    for j in range(2):
        shift = lam_ref[j] * n
        for p in range(NB):
            for q in range(p, NB):
                v = jnp.concatenate([a_ref[s, IDX[p, q]] for s in range(8)], axis=0)
                if p == q:
                    v = v + jnp.where(row == col, shift, 0.0)
                s_ref[j, p, :, 128 * q:128 * q + 128] = v
        for s in range(8):
            for q in range(NB):
                y_ref[j, s:s + 1, 128 * q:128 * q + 128] = a_ref[s, 10, q:q + 1, :]
    for p in range(NB):
        lo, hi = 128 * p, 128 * p + 128
        ws = inverse([s_ref[j, p, :, lo:hi] for j in range(2)])
        for j in range(2):
            w = ws[j]
            y = dot(y_ref[j, :, lo:hi], w)
            y_ref[j, :, lo:hi] = y
            if p + 1 < NB:
                right = s_ref[j, p, :, hi:]
                t = dot(w, right)
                t_ref[j, p, :, hi:] = t
                y_ref[j, :, hi:] = y_ref[j, :, hi:] - dot(y, right)
                for q in range(p + 1, NB):
                    k = 128 * q
                    s_ref[j, q, :, k:] = s_ref[j, q, :, k:] - dot(s_ref[j, p, :, k:k + 128], t_ref[j, p, :, k:], 0, 0)
    for j in range(2):
        for p in range(NB - 2, -1, -1):
            lo, hi = 128 * p, 128 * p + 128
            y_ref[j, :, lo:hi] = y_ref[j, :, lo:hi] - dot(y_ref[j, :, hi:], t_ref[j, p, :, hi:], 1, 1)
    for t in range(8):
        for j in range(2):
            x_ref[2 * t + j:2 * t + j + 1, :] = y_ref[j, t:t + 1, :]
    out_ref[...] = x_ref[...].astype(jnp.bfloat16)


def solve(lam, a):
    return pl.pallas_call(
        solve_kernel,
        out_shape=jax.ShapeDtypeStruct((16, 512), jnp.bfloat16),
        in_specs=[pl.BlockSpec(memory_space=pltpu.SMEM), pl.BlockSpec(memory_space=pltpu.VMEM)],
        out_specs=pl.BlockSpec(memory_space=pltpu.VMEM),
        scratch_shapes=[pltpu.VMEM((2, 4, 128, 512), jnp.float32), pltpu.VMEM((2, 4, 128, 512), jnp.float32), pltpu.VMEM((2, 8, 512), jnp.float32), pltpu.VMEM((16, 512), jnp.float32)],
        compiler_params=pltpu.CompilerParams(vmem_limit_bytes=40 << 20),
    )(lam, a)


MESH = pl.DeviceIdType.MESH
FOLDS = 5
BLOCK = 512
TRAITS = 8
SLOTS = 11


def to_smp(device):
    return {"smp": device}


def gram_kernel(x_ref, yt_ref, fold_ref, out_ref, lhs, part, relay, plain, comb, half, zin, done, send, recv, gsend, grecv):
    me = lax.axis_index("smp")
    y, z = lax.div(me, 2), lax.rem(me, 2)
    right = lax.rem(y + 1, 4) * 2 + z
    left = lax.rem(y + 3, 4) * 2 + z
    across = lax.rem(y + 2, 4)
    other = y * 2 + (1 - z)
    barrier = pltpu.get_barrier_semaphore()

    def greet(i, carry):
        pl.semaphore_signal(barrier, inc=1, device_id=to_smp(lax.rem(me + i, 8)), device_id_type=MESH)
        return carry

    lax.fori_loop(1, 8, greet, 0)

    @pl.when(me >= FOLDS)
    def _():
        out_ref[...] = jnp.zeros_like(out_ref)

    lhs[0:256, :] = jnp.transpose(x_ref[:, 0:256])
    lhs[256:272, :] = yt_ref[...]
    lhs[272:528, :] = jnp.transpose(x_ref[:, 256:512])

    def hop(kind, k, src, dst, device):
        return pltpu.make_async_remote_copy(
            src_ref=src, dst_ref=dst, send_sem=send.at[kind, k], recv_sem=recv.at[kind, k],
            device_id=to_smp(device), device_id_type=MESH)

    def relays(k):
        return [hop(0, k, part.at[across * 2, k], relay.at[0, k], right),
                hop(1, k, part.at[across * 2 + 1, k], relay.at[1, k], left)]

    def plains(k):
        return [hop(2, k, part.at[lax.rem(y + 1, 4) * 2 + 1, k], plain.at[0, k], right),
                hop(3, k, part.at[lax.rem(y + 3, 4) * 2, k], plain.at[1, k], left)]

    def combs(k):
        return [hop(4, k, relay.at[0, k], comb.at[0, k], right),
                hop(5, k, relay.at[1, k], comb.at[1, k], left)]

    def cross_z(k):
        return hop(6, k, half.at[k], zin.at[k], other)

    def gather(k):
        return pltpu.make_async_remote_copy(
            src_ref=done.at[k], dst_ref=out_ref.at[me], send_sem=gsend.at[k], recv_sem=grecv.at[me],
            device_id=to_smp(k), device_id_type=MESH)

    def products(k):
        mask = jnp.where(fold_ref[...] != k, 1.0, 0.0).astype(jnp.bfloat16)
        top = jnp.dot(lhs[0:272, :] * mask, x_ref[...], preferred_element_type=jnp.float32)
        low = jnp.dot(lhs[272:528, :] * mask, x_ref[:, 256:512], preferred_element_type=jnp.float32)
        for s in range(8):
            slot = 0
            for p in range(4):
                for q in range(p, 4):
                    r = 128 * p + 16 * s
                    if p < 2:
                        v = top[r:r + 16, 128 * q:128 * q + 128]
                    else:
                        v = low[r - 256:r - 240, 128 * q - 256:128 * q - 128]
                    part[s, k, slot] = v
                    slot += 1
            for q in range(4):
                part[s, k, slot, q:q + 1, :] = top[256 + s:257 + s, 128 * q:128 * q + 128]
            part[s, k, slot, 4:16, :] = jnp.zeros((12, 128), jnp.float32)

    def step(i, carry):
        @pl.when(i < FOLDS)
        def _():
            products(i)

            @pl.when(i == 0)
            def _():
                pl.semaphore_wait(barrier, 7)

            for c in relays(i):
                c.start()
            for c in plains(i):
                c.start()

        @pl.when((i >= 1) & (i < 1 + FOLDS))
        def _():
            k = i - 1
            for c in relays(k):
                c.wait_recv()
            relay[0, k] += part[lax.rem(y + 1, 4) * 2, k]
            relay[1, k] += part[lax.rem(y + 3, 4) * 2 + 1, k]
            for c in combs(k):
                c.start()

        @pl.when((i >= 3) & (i < 3 + FOLDS))
        def _():
            k = i - 3
            for c in plains(k) + combs(k):
                c.wait_recv()
            zero = part[y * 2, k] + plain[1, k] + comb[0, k]
            one = part[y * 2 + 1, k] + plain[0, k] + comb[1, k]
            half[k] = jnp.where(z == 0, one, zero)
            done[k] = jnp.where(z == 0, zero, one)
            cross_z(k).start()

        @pl.when(i >= 5)
        def _():
            k = i - 5
            cross_z(k).wait_recv()
            done[k] += zin[k]

            @pl.when(me != k)
            def _():
                gather(k).start()

            @pl.when(me == k)
            def _():
                out_ref[me] = done[k]

        return carry

    lax.fori_loop(0, 5 + FOLDS, step, 0)

    def finish(k, carry):
        for c in relays(k) + plains(k) + combs(k):
            c.wait_send()
        cross_z(k).wait_send()

        @pl.when(me != k)
        def _():
            gather(k).wait_send()

        return carry

    lax.fori_loop(0, FOLDS, finish, 0)

    @pl.when(me < FOLDS)
    def _():
        def arrive(i, carry):
            s = lax.rem(me + i, 8)
            pltpu.make_async_remote_copy(
                src_ref=done.at[0], dst_ref=out_ref.at[s], send_sem=gsend.at[0], recv_sem=grecv.at[s],
                device_id=to_smp(s), device_id_type=MESH).wait_recv()
            return carry

        lax.fori_loop(1, 8, arrive, 0)


def gram_sums(x, yt, fold):
    piece = (SLOTS, 16, 128)
    vmem = pl.BlockSpec(memory_space=pltpu.VMEM)
    f32 = jnp.float32
    return pl.pallas_call(
        gram_kernel,
        out_shape=jax.ShapeDtypeStruct((8,) + piece, f32),
        in_specs=[vmem] * 3,
        out_specs=vmem,
        scratch_shapes=[
            pltpu.VMEM((528, x.shape[0]), jnp.bfloat16),
            pltpu.VMEM((8, FOLDS) + piece, f32),
            pltpu.VMEM((2, FOLDS) + piece, f32),
            pltpu.VMEM((2, FOLDS) + piece, f32),
            pltpu.VMEM((2, FOLDS) + piece, f32),
            pltpu.VMEM((FOLDS,) + piece, f32),
            pltpu.VMEM((FOLDS,) + piece, f32),
            pltpu.VMEM((FOLDS,) + piece, f32),
            pltpu.SemaphoreType.DMA((7, FOLDS)),
            pltpu.SemaphoreType.DMA((7, FOLDS)),
            pltpu.SemaphoreType.DMA((FOLDS,)),
            pltpu.SemaphoreType.DMA((8,)),
        ],
        compiler_params=pltpu.CompilerParams(collective_id=1, has_side_effects=True, vmem_limit_bytes=40 << 20),
    )(x, yt, fold)


def tail_kernel(beta_ref, x_ref, fold_ref, old_ref, oof_ref, cross_ref, betas, mine, feats, terms, rows, sums,
                bsend, brecv, fsend, frecv, tsend, trecv, ssend, srecv):
    s, b = lax.axis_index("smp"), lax.axis_index("blk")
    samples = x_ref.shape[0]
    barrier = pltpu.get_barrier_semaphore()

    def greet_smp(i, carry):
        pl.semaphore_signal(barrier, inc=1, device_id={"smp": lax.rem(s + i, 8)}, device_id_type=MESH)
        return carry

    def greet_blk(i, carry):
        pl.semaphore_signal(barrier, inc=1, device_id={"blk": lax.rem(b + i, 16)}, device_id_type=MESH)
        return carry

    lax.fori_loop(1, 8, greet_smp, 0)
    lax.fori_loop(1, 16, greet_blk, 0)
    pl.semaphore_wait(barrier, 22)

    def spread(i):
        return pltpu.make_async_remote_copy(
            src_ref=beta_ref, dst_ref=betas.at[s], send_sem=bsend.at[i], recv_sem=brecv.at[s],
            device_id={"smp": lax.rem(s + i, 8)}, device_id_type=MESH)

    def start_spread(i, carry):
        spread(i).start()
        return carry

    def end_spread(i, carry):
        spread(i).wait_send()
        return carry

    @pl.when(s < FOLDS)
    def _():
        lax.fori_loop(1, 8, start_spread, 0)
        betas[s] = beta_ref[...]

    def beta_in(k, carry):
        @pl.when(s != k)
        def _():
            pltpu.make_async_remote_copy(
                src_ref=beta_ref, dst_ref=betas.at[k], send_sem=bsend.at[0], recv_sem=brecv.at[k],
                device_id={"smp": k}, device_id_type=MESH).wait_recv()
        return carry

    lax.fori_loop(0, FOLDS, beta_in, 0)
    flat = jnp.concatenate([betas[k] for k in range(FOLDS)], axis=0)
    fitted = lax.dot_general(flat, x_ref[...], (((1,), (1,)), ((), ())), preferred_element_type=jnp.float32)
    fold = fold_ref[...]
    chosen = jnp.zeros((16, samples), jnp.float32)
    for k in range(FOLDS):
        chosen = jnp.where(fold == k, fitted[16 * k:16 * k + 16, :], chosen)
    oof = (chosen * math.sqrt(8 * samples / BLOCK)).astype(jnp.bfloat16)
    oof_ref[...] = oof
    for c in range(16):
        mine[c] = oof[:, 128 * c:128 * c + 128]
    feats[b] = mine[b]

    def feature(i):
        to = lax.rem(b + i, 16)
        return pltpu.make_async_remote_copy(
            src_ref=mine.at[to], dst_ref=feats.at[b], send_sem=fsend.at[i], recv_sem=frecv.at[i],
            device_id={"blk": to}, device_id_type=MESH)

    def start_feature(i, carry):
        feature(i).start()
        return carry

    def end_feature(i, carry):
        feature(i).wait()
        return carry

    lax.fori_loop(1, 16, start_feature, 0)
    lax.fori_loop(1, 16, end_feature, 0)
    f = jnp.concatenate([feats[c] for c in range(16)], axis=0)
    nt = (((1,), (1,)), ((), ()))
    against_old = lax.dot_general(f, old_ref[...], nt, preferred_element_type=jnp.float32)
    against_new = lax.dot_general(f, f, nt, preferred_element_type=jnp.float32)
    r = lax.broadcasted_iota(jnp.int32, (256, 256), 0)
    c = lax.broadcasted_iota(jnp.int32, (256, 256), 1)
    row_trait = (r >> 1) & 7
    against_old = jnp.where(row_trait == (c >> 5), against_old, 0.0)
    against_new = jnp.where(row_trait == ((c >> 1) & 7), against_new, 0.0)
    r = lax.broadcasted_iota(jnp.int32, (256, 128), 0)
    c = lax.broadcasted_iota(jnp.int32, (256, 128), 1)
    pick_old = jnp.where((r & 31) == c, 1.0, 0.0)
    pick_new = jnp.where(32 + ((r >> 4) << 1) + (r & 1) == c, 1.0, 0.0)
    total = dot(against_old, pick_old) + dot(against_new, pick_new)
    for k in range(16):
        terms[k] = total[16 * k:16 * k + 16, :]
    rows[b] = terms[b]

    def term(i):
        to = lax.rem(b + i, 16)
        return pltpu.make_async_remote_copy(
            src_ref=terms.at[to], dst_ref=rows.at[b], send_sem=tsend.at[i], recv_sem=trecv.at[i],
            device_id={"blk": to}, device_id_type=MESH)

    def start_term(i, carry):
        term(i).start()
        return carry

    def end_term(i, carry):
        term(i).wait()
        return carry

    lax.fori_loop(1, 16, start_term, 0)
    lax.fori_loop(1, 16, end_term, 0)
    part = rows[0]
    for k in range(1, 16):
        part = part + rows[k]
    sums[s] = part

    def last(i):
        return pltpu.make_async_remote_copy(
            src_ref=sums.at[s], dst_ref=sums.at[s], send_sem=ssend.at[i], recv_sem=srecv.at[i],
            device_id={"smp": lax.rem(s + i, 8)}, device_id_type=MESH)

    def start_last(i, carry):
        last(i).start()
        return carry

    def end_last(i, carry):
        last(i).wait()
        return carry

    lax.fori_loop(1, 8, start_last, 0)
    lax.fori_loop(1, 8, end_last, 0)
    final = sums[0]
    for k in range(1, 8):
        final = final + sums[k]
    cross_ref[...] = final * (1.0 / (8 * samples))

    @pl.when(s < FOLDS)
    def _():
        lax.fori_loop(1, 8, end_spread, 0)


def tail(beta, x, fold, old):
    vmem = pl.BlockSpec(memory_space=pltpu.VMEM)
    dma = pltpu.SemaphoreType.DMA
    return pl.pallas_call(
        tail_kernel,
        out_shape=(jax.ShapeDtypeStruct((16, x.shape[0]), jnp.bfloat16), jax.ShapeDtypeStruct((16, 128), jnp.float32)),
        in_specs=[vmem] * 4,
        out_specs=(vmem, vmem),
        scratch_shapes=[
            pltpu.VMEM((FOLDS, 16, BLOCK), jnp.bfloat16),
            pltpu.VMEM((16, 16, 128), jnp.bfloat16),
            pltpu.VMEM((16, 16, 128), jnp.bfloat16),
            pltpu.VMEM((16, 16, 128), jnp.float32),
            pltpu.VMEM((16, 16, 128), jnp.float32),
            pltpu.VMEM((8, 16, 128), jnp.float32),
            dma((8,)), dma((8,)), dma((16,)), dma((16,)), dma((16,)), dma((16,)), dma((8,)), dma((8,)),
        ],
        compiler_params=pltpu.CompilerParams(collective_id=2, has_side_effects=True, vmem_limit_bytes=40 << 20),
    )(beta, x, fold, old)


def local(x, y, fold, lam, old):
    rows = x.shape[0]
    fold = fold[None, :]
    yt = jnp.pad(y.T, ((0, 8), (0, 0)))
    pieces = gram_sums(x, yt, fold)
    beta = solve(lam, pieces)
    before = jnp.transpose(old[0], (1, 2, 0)).reshape(256, 128)
    oof, cross = tail(beta, x, fold, before)
    here = lax.dynamic_slice_in_dim(cross, 8 * lax.axis_index("smp"), 8, 1)
    return jnp.transpose(oof.reshape(TRAITS, 2, rows), (2, 0, 1)), here.reshape(TRAITS, 2, 8)


def solution(mesh):
    return jax.shard_map(
        local,
        mesh=mesh,
        in_specs=(P("smp", "blk"), P("smp", None), P("smp"), P(), P("smp", "blk", None, None)),
        out_specs=(P("smp", None, "blk"), P(None, "blk", "smp")),
        check_vma=False,
    )
```

```python
import math

import jax
import jax.numpy as jnp
from jax import lax
from jax.experimental import pallas as pl
from jax.experimental.pallas import tpu as pltpu
from jax.sharding import PartitionSpec as P

HI = lax.Precision.HIGHEST
NB = 4
BLK = [(p, q) for p in range(NB) for q in range(p, NB)]
IDX = {pq: i for i, pq in enumerate(BLK)}


def lanes(x, m):
    return jnp.broadcast_to(x[:, m:m + 1], x.shape)


def subl(x, m):
    return jnp.broadcast_to(x[m:m + 1, :], x.shape)


def split3(x):
    hi = x.astype(jnp.bfloat16).astype(jnp.float32)
    r = x - hi
    mid = r.astype(jnp.bfloat16).astype(jnp.float32)
    return hi, mid, r - mid


def pivots(a0, base, lane, sub):
    cols = [lanes(a0, base + m) for m in range(8)]
    inside = (lane >= base) & (lane < base + 8)
    z = jnp.where(inside, jnp.where(lane - base == sub, -1.0, 0.0), a0)
    scale = None
    for m in range(8):
        d = 1.0 / subl(cols[m], m)
        l = jnp.where(sub == m, 0.0, cols[m] * d)
        z = z - l * subl(z, m)
        for j in range(m + 1, 8):
            cols[j] = cols[j] - l * subl(cols[j], m)
        scale = d if m == 0 else jnp.where(sub == m, d, scale)
    return z * scale, inside


def inverse(mats):
    n = len(mats)
    lane = lax.broadcasted_iota(jnp.int32, (8, 128), 1)
    sub = lax.broadcasted_iota(jnp.int32, (8, 128), 0)
    mats = [[a[8*i:8*i+8] for i in range(16)] for a in mats]
    for g in range(16):
        for t in range(n):
            a = mats[t]
            base = 8 * g
            a0 = a[g]
            qs, inside = pivots(a0, base, lane, sub)
            h, m, l = split3(a0)
            lhs = jnp.concatenate([h, h, m, h, l, m], axis=0).astype(jnp.bfloat16)
            h, m, l = split3(qs)
            rhs = jnp.concatenate([h, m, h, l, h, m], axis=0).astype(jnp.bfloat16)
            upd = lax.dot_general(lhs, rhs, (((0,), (0,)), ((), ())), preferred_element_type=jnp.float32)
            new = []
            for i in range(16):
                if i == g:
                    v = qs
                elif i == g + 1:
                    v = jnp.where(inside, 0.0, a[i])
                    t1 = v - lanes(a[i], base) * subl(qs, 0)
                    t2 = lanes(a[i], base + 1) * subl(qs, 1)
                    for m in range(2, 8, 2):
                        t1 = t1 - lanes(a[i], base + m) * subl(qs, m)
                        t2 = t2 + lanes(a[i], base + m + 1) * subl(qs, m + 1)
                    v = t1 - t2
                else:
                    v = jnp.where(inside, 0.0, a[i]) - upd[8*i:8*i+8]
                new.append(v)
            mats[t] = new
    return [-jnp.concatenate(a, axis=0) for a in mats]


def dot(a, b, ca=1, cb=0):
    return lax.dot_general(a, b, (((ca,), (cb,)), ((), ())), precision=HI, preferred_element_type=jnp.float32)


def solve_kernel(lam_ref, a_ref, out_ref, s_ref, t_ref, y_ref, x_ref):
    n = 16384.0
    row = lax.broadcasted_iota(jnp.int32, (128, 128), 0)
    col = lax.broadcasted_iota(jnp.int32, (128, 128), 1)
    for j in range(2):
        shift = lam_ref[j] * n
        for p in range(NB):
            for q in range(p, NB):
                v = jnp.concatenate([a_ref[s, IDX[p, q]] for s in range(8)], axis=0)
                if p == q:
                    v = v + jnp.where(row == col, shift, 0.0)
                s_ref[j, p, :, 128 * q:128 * q + 128] = v
        for s in range(8):
            for q in range(NB):
                y_ref[j, s:s + 1, 128 * q:128 * q + 128] = a_ref[s, 10, q:q + 1, :]
    for p in range(NB):
        lo, hi = 128 * p, 128 * p + 128
        ws = inverse([s_ref[j, p, :, lo:hi] for j in range(2)])
        for j in range(2):
            w = ws[j]
            y = dot(y_ref[j, :, lo:hi], w)
            y_ref[j, :, lo:hi] = y
            if p + 1 < NB:
                right = s_ref[j, p, :, hi:]
                t = dot(w, right)
                t_ref[j, p, :, hi:] = t
                y_ref[j, :, hi:] = y_ref[j, :, hi:] - dot(y, right)
                for q in range(p + 1, NB):
                    k = 128 * q
                    s_ref[j, q, :, k:] = s_ref[j, q, :, k:] - dot(s_ref[j, p, :, k:k + 128], t_ref[j, p, :, k:], 0, 0)
    for j in range(2):
        for p in range(NB - 2, -1, -1):
            lo, hi = 128 * p, 128 * p + 128
            y_ref[j, :, lo:hi] = y_ref[j, :, lo:hi] - dot(y_ref[j, :, hi:], t_ref[j, p, :, hi:], 1, 1)
    for t in range(8):
        for j in range(2):
            x_ref[2 * t + j:2 * t + j + 1, :] = y_ref[j, t:t + 1, :]
    out_ref[...] = x_ref[...].astype(jnp.bfloat16)


def solve(lam, a):
    return pl.pallas_call(
        solve_kernel,
        out_shape=jax.ShapeDtypeStruct((16, 512), jnp.bfloat16),
        in_specs=[pl.BlockSpec(memory_space=pltpu.SMEM), pl.BlockSpec(memory_space=pltpu.VMEM)],
        out_specs=pl.BlockSpec(memory_space=pltpu.VMEM),
        scratch_shapes=[pltpu.VMEM((2, 4, 128, 512), jnp.float32), pltpu.VMEM((2, 4, 128, 512), jnp.float32), pltpu.VMEM((2, 8, 512), jnp.float32), pltpu.VMEM((16, 512), jnp.float32)],
        compiler_params=pltpu.CompilerParams(vmem_limit_bytes=40 << 20),
    )(lam, a)


MESH = pl.DeviceIdType.MESH
FOLDS = 5
BLOCK = 512
TRAITS = 8
SLOTS = 11


def to_smp(device):
    return {"smp": device}


def gram_kernel(x_ref, yt_ref, fold_ref, out_ref, lhs, part, relay, plain, comb, half, zin, done, send, recv, gsend, grecv):
    me = lax.axis_index("smp")
    y, z = lax.div(me, 2), lax.rem(me, 2)
    right = lax.rem(y + 1, 4) * 2 + z
    left = lax.rem(y + 3, 4) * 2 + z
    across = lax.rem(y + 2, 4)
    other = y * 2 + (1 - z)
    barrier = pltpu.get_barrier_semaphore()

    def greet(i, carry):
        pl.semaphore_signal(barrier, inc=1, device_id=to_smp(lax.rem(me + i, 8)), device_id_type=MESH)
        return carry

    lax.fori_loop(1, 8, greet, 0)

    @pl.when(me >= FOLDS)
    def _():
        out_ref[...] = jnp.zeros_like(out_ref)

    lhs[0:256, :] = jnp.transpose(x_ref[:, 0:256])
    lhs[256:272, :] = yt_ref[...]
    lhs[272:528, :] = jnp.transpose(x_ref[:, 256:512])

    def hop(kind, k, src, dst, device):
        return pltpu.make_async_remote_copy(
            src_ref=src, dst_ref=dst, send_sem=send.at[kind, k], recv_sem=recv.at[kind, k],
            device_id=to_smp(device), device_id_type=MESH)

    def relays(k):
        return [hop(0, k, part.at[across * 2, k], relay.at[0, k], right),
                hop(1, k, part.at[across * 2 + 1, k], relay.at[1, k], left)]

    def plains(k):
        return [hop(2, k, part.at[lax.rem(y + 1, 4) * 2 + 1, k], plain.at[0, k], right),
                hop(3, k, part.at[lax.rem(y + 3, 4) * 2, k], plain.at[1, k], left)]

    def combs(k):
        return [hop(4, k, relay.at[0, k], comb.at[0, k], right),
                hop(5, k, relay.at[1, k], comb.at[1, k], left)]

    def cross_z(k):
        return hop(6, k, half.at[k], zin.at[k], other)

    def gather(k):
        return pltpu.make_async_remote_copy(
            src_ref=done.at[k], dst_ref=out_ref.at[me], send_sem=gsend.at[k], recv_sem=grecv.at[me],
            device_id=to_smp(k), device_id_type=MESH)

    def products(k):
        mask = jnp.where(fold_ref[...] != k, 1.0, 0.0).astype(jnp.bfloat16)
        top = jnp.dot(lhs[0:272, :] * mask, x_ref[...], preferred_element_type=jnp.float32)
        low = jnp.dot(lhs[272:528, :] * mask, x_ref[:, 256:512], preferred_element_type=jnp.float32)
        for s in range(8):
            slot = 0
            for p in range(4):
                for q in range(p, 4):
                    r = 128 * p + 16 * s
                    if p < 2:
                        v = top[r:r + 16, 128 * q:128 * q + 128]
                    else:
                        v = low[r - 256:r - 240, 128 * q - 256:128 * q - 128]
                    part[s, k, slot] = v
                    slot += 1
            for q in range(4):
                part[s, k, slot, q:q + 1, :] = top[256 + s:257 + s, 128 * q:128 * q + 128]
            part[s, k, slot, 4:16, :] = jnp.zeros((12, 128), jnp.float32)

    def step(i, carry):
        @pl.when(i < FOLDS)
        def _():
            products(i)

            @pl.when(i == 0)
            def _():
                pl.semaphore_wait(barrier, 7)

            for c in relays(i):
                c.start()
            for c in plains(i):
                c.start()

        @pl.when((i >= 1) & (i < 1 + FOLDS))
        def _():
            k = i - 1
            for c in relays(k):
                c.wait_recv()
            relay[0, k] += part[lax.rem(y + 1, 4) * 2, k]
            relay[1, k] += part[lax.rem(y + 3, 4) * 2 + 1, k]
            for c in combs(k):
                c.start()

        @pl.when((i >= 3) & (i < 3 + FOLDS))
        def _():
            k = i - 3
            for c in plains(k) + combs(k):
                c.wait_recv()
            zero = part[y * 2, k] + plain[1, k] + comb[0, k]
            one = part[y * 2 + 1, k] + plain[0, k] + comb[1, k]
            half[k] = jnp.where(z == 0, one, zero)
            done[k] = jnp.where(z == 0, zero, one)
            cross_z(k).start()

        @pl.when(i >= 5)
        def _():
            k = i - 5
            cross_z(k).wait_recv()
            done[k] += zin[k]

            @pl.when(me != k)
            def _():
                gather(k).start()

            @pl.when(me == k)
            def _():
                out_ref[me] = done[k]

        return carry

    lax.fori_loop(0, 5 + FOLDS, step, 0)

    def finish(k, carry):
        for c in relays(k) + plains(k) + combs(k):
            c.wait_send()
        cross_z(k).wait_send()

        @pl.when(me != k)
        def _():
            gather(k).wait_send()

        return carry

    lax.fori_loop(0, FOLDS, finish, 0)

    @pl.when(me < FOLDS)
    def _():
        def arrive(i, carry):
            s = lax.rem(me + i, 8)
            pltpu.make_async_remote_copy(
                src_ref=done.at[0], dst_ref=out_ref.at[s], send_sem=gsend.at[0], recv_sem=grecv.at[s],
                device_id=to_smp(s), device_id_type=MESH).wait_recv()
            return carry

        lax.fori_loop(1, 8, arrive, 0)


def gram_sums(x, yt, fold):
    piece = (SLOTS, 16, 128)
    vmem = pl.BlockSpec(memory_space=pltpu.VMEM)
    f32 = jnp.float32
    return pl.pallas_call(
        gram_kernel,
        out_shape=jax.ShapeDtypeStruct((8,) + piece, f32),
        in_specs=[vmem] * 3,
        out_specs=vmem,
        scratch_shapes=[
            pltpu.VMEM((528, x.shape[0]), jnp.bfloat16),
            pltpu.VMEM((8, FOLDS) + piece, f32),
            pltpu.VMEM((2, FOLDS) + piece, f32),
            pltpu.VMEM((2, FOLDS) + piece, f32),
            pltpu.VMEM((2, FOLDS) + piece, f32),
            pltpu.VMEM((FOLDS,) + piece, f32),
            pltpu.VMEM((FOLDS,) + piece, f32),
            pltpu.VMEM((FOLDS,) + piece, f32),
            pltpu.SemaphoreType.DMA((7, FOLDS)),
            pltpu.SemaphoreType.DMA((7, FOLDS)),
            pltpu.SemaphoreType.DMA((FOLDS,)),
            pltpu.SemaphoreType.DMA((8,)),
        ],
        compiler_params=pltpu.CompilerParams(collective_id=1, has_side_effects=True, vmem_limit_bytes=40 << 20),
    )(x, yt, fold)


def tail_kernel(beta_ref, x_ref, fold_ref, old_ref, oof_ref, cross_ref, betas, mine, feats, terms, rows, sums,
                bsend, brecv, fsend, frecv, tsend, trecv, ssend, srecv):
    s, b = lax.axis_index("smp"), lax.axis_index("blk")
    samples = x_ref.shape[0]
    barrier = pltpu.get_barrier_semaphore()

    def greet_smp(i, carry):
        pl.semaphore_signal(barrier, inc=1, device_id={"smp": lax.rem(s + i, 8)}, device_id_type=MESH)
        return carry

    def greet_blk(i, carry):
        pl.semaphore_signal(barrier, inc=1, device_id={"blk": lax.rem(b + i, 16)}, device_id_type=MESH)
        return carry

    lax.fori_loop(1, 8, greet_smp, 0)
    lax.fori_loop(1, 16, greet_blk, 0)
    pl.semaphore_wait(barrier, 22)

    def spread(i):
        return pltpu.make_async_remote_copy(
            src_ref=beta_ref, dst_ref=betas.at[s], send_sem=bsend.at[i], recv_sem=brecv.at[s],
            device_id={"smp": lax.rem(s + i, 8)}, device_id_type=MESH)

    def start_spread(i, carry):
        spread(i).start()
        return carry

    def end_spread(i, carry):
        spread(i).wait_send()
        return carry

    @pl.when(s < FOLDS)
    def _():
        lax.fori_loop(1, 8, start_spread, 0)
        betas[s] = beta_ref[...]

    def beta_in(k, carry):
        @pl.when(s != k)
        def _():
            pltpu.make_async_remote_copy(
                src_ref=beta_ref, dst_ref=betas.at[k], send_sem=bsend.at[0], recv_sem=brecv.at[k],
                device_id={"smp": k}, device_id_type=MESH).wait_recv()
        return carry

    lax.fori_loop(0, FOLDS, beta_in, 0)
    flat = jnp.concatenate([betas[k] for k in range(FOLDS)], axis=0)
    fitted = lax.dot_general(flat, x_ref[...], (((1,), (1,)), ((), ())), preferred_element_type=jnp.float32)
    fold = fold_ref[...]
    chosen = jnp.zeros((16, samples), jnp.float32)
    for k in range(FOLDS):
        chosen = jnp.where(fold == k, fitted[16 * k:16 * k + 16, :], chosen)
    oof = (chosen * math.sqrt(8 * samples / BLOCK)).astype(jnp.bfloat16)
    oof_ref[...] = oof
    for c in range(16):
        mine[c] = oof[:, 128 * c:128 * c + 128]
    feats[b] = mine[b]

    def feature(i):
        to = lax.rem(b + i, 16)
        return pltpu.make_async_remote_copy(
            src_ref=mine.at[to], dst_ref=feats.at[b], send_sem=fsend.at[i], recv_sem=frecv.at[i],
            device_id={"blk": to}, device_id_type=MESH)

    def start_feature(i, carry):
        feature(i).start()
        return carry

    def end_feature(i, carry):
        feature(i).wait()
        return carry

    lax.fori_loop(1, 16, start_feature, 0)
    lax.fori_loop(1, 16, end_feature, 0)
    f = jnp.concatenate([feats[c] for c in range(16)], axis=0)
    nt = (((1,), (1,)), ((), ()))
    against_old = lax.dot_general(f, old_ref[...], nt, preferred_element_type=jnp.float32)
    against_new = lax.dot_general(f, f, nt, preferred_element_type=jnp.float32)
    r = lax.broadcasted_iota(jnp.int32, (256, 256), 0)
    c = lax.broadcasted_iota(jnp.int32, (256, 256), 1)
    row_trait = (r >> 1) & 7
    against_old = jnp.where(row_trait == (c >> 5), against_old, 0.0)
    against_new = jnp.where(row_trait == ((c >> 1) & 7), against_new, 0.0)
    r = lax.broadcasted_iota(jnp.int32, (256, 128), 0)
    c = lax.broadcasted_iota(jnp.int32, (256, 128), 1)
    pick_old = jnp.where((r & 31) == c, 1.0, 0.0)
    pick_new = jnp.where(32 + ((r >> 4) << 1) + (r & 1) == c, 1.0, 0.0)
    total = dot(against_old, pick_old) + dot(against_new, pick_new)
    for k in range(16):
        terms[k] = total[16 * k:16 * k + 16, :]
    rows[b] = terms[b]

    def term(i):
        to = lax.rem(b + i, 16)
        return pltpu.make_async_remote_copy(
            src_ref=terms.at[to], dst_ref=rows.at[b], send_sem=tsend.at[i], recv_sem=trecv.at[i],
            device_id={"blk": to}, device_id_type=MESH)

    def start_term(i, carry):
        term(i).start()
        return carry

    def end_term(i, carry):
        term(i).wait()
        return carry

    lax.fori_loop(1, 16, start_term, 0)
    lax.fori_loop(1, 16, end_term, 0)
    part = rows[0]
    for k in range(1, 16):
        part = part + rows[k]
    sums[s] = part

    def last(i):
        return pltpu.make_async_remote_copy(
            src_ref=sums.at[s], dst_ref=sums.at[s], send_sem=ssend.at[i], recv_sem=srecv.at[i],
            device_id={"smp": lax.rem(s + i, 8)}, device_id_type=MESH)

    def start_last(i, carry):
        last(i).start()
        return carry

    def end_last(i, carry):
        last(i).wait()
        return carry

    lax.fori_loop(1, 8, start_last, 0)
    lax.fori_loop(1, 8, end_last, 0)
    final = sums[0]
    for k in range(1, 8):
        final = final + sums[k]
    cross_ref[...] = final * (1.0 / (8 * samples))

    @pl.when(s < FOLDS)
    def _():
        lax.fori_loop(1, 8, end_spread, 0)


def tail(beta, x, fold, old):
    vmem = pl.BlockSpec(memory_space=pltpu.VMEM)
    dma = pltpu.SemaphoreType.DMA
    return pl.pallas_call(
        tail_kernel,
        out_shape=(jax.ShapeDtypeStruct((16, x.shape[0]), jnp.bfloat16), jax.ShapeDtypeStruct((16, 128), jnp.float32)),
        in_specs=[vmem] * 4,
        out_specs=(vmem, vmem),
        scratch_shapes=[
            pltpu.VMEM((FOLDS, 16, BLOCK), jnp.bfloat16),
            pltpu.VMEM((16, 16, 128), jnp.bfloat16),
            pltpu.VMEM((16, 16, 128), jnp.bfloat16),
            pltpu.VMEM((16, 16, 128), jnp.float32),
            pltpu.VMEM((16, 16, 128), jnp.float32),
            pltpu.VMEM((8, 16, 128), jnp.float32),
            dma((8,)), dma((8,)), dma((16,)), dma((16,)), dma((16,)), dma((16,)), dma((8,)), dma((8,)),
        ],
        compiler_params=pltpu.CompilerParams(collective_id=2, has_side_effects=True, vmem_limit_bytes=40 << 20),
    )(beta, x, fold, old)


def local(x, y, fold, lam, old):
    rows = x.shape[0]
    fold = fold[None, :]
    yt = jnp.pad(y.T, ((0, 8), (0, 0)))
    pieces = gram_sums(x, yt, fold)
    beta = solve(lam, pieces)
    before = jnp.transpose(old[0], (1, 2, 0)).reshape(256, 128)
    oof, cross = tail(beta, x, fold, before)
    here = lax.dynamic_slice_in_dim(cross, 8 * lax.axis_index("smp"), 8, 1)
    return jnp.transpose(oof.reshape(TRAITS, 2, rows), (2, 0, 1)), here.reshape(TRAITS, 2, 8)


def solution(mesh):
    return jax.shard_map(
        local,
        mesh=mesh,
        in_specs=(P("smp", "blk"), P("smp", None), P("smp"), P(), P("smp", "blk", None, None)),
        out_specs=(P("smp", None, "blk"), P(None, "blk", "smp")),
        check_vma=False,
    )
```

```python
import math

import jax
import jax.numpy as jnp
from jax import lax
from jax.experimental import pallas as pl
from jax.experimental.pallas import tpu as pltpu
from jax.sharding import PartitionSpec as P

HI = lax.Precision.HIGHEST
NB = 4
BLK = [(p, q) for p in range(NB) for q in range(p, NB)]
IDX = {pq: i for i, pq in enumerate(BLK)}


def lanes(x, m):
    return jnp.broadcast_to(x[:, m:m + 1], x.shape)


def subl(x, m):
    return jnp.broadcast_to(x[m:m + 1, :], x.shape)


def split3(x):
    hi = x.astype(jnp.bfloat16).astype(jnp.float32)
    r = x - hi
    mid = r.astype(jnp.bfloat16).astype(jnp.float32)
    return hi, mid, r - mid


def pivots(a0, base, lane, sub):
    cols = [lanes(a0, base + m) for m in range(8)]
    inside = (lane >= base) & (lane < base + 8)
    z = jnp.where(inside, jnp.where(lane - base == sub, -1.0, 0.0), a0)
    scale = None
    for m in range(8):
        d = 1.0 / subl(cols[m], m)
        l = jnp.where(sub == m, 0.0, cols[m] * d)
        z = z - l * subl(z, m)
        for j in range(m + 1, 8):
            cols[j] = cols[j] - l * subl(cols[j], m)
        scale = d if m == 0 else jnp.where(sub == m, d, scale)
    return z * scale, inside


def inverse(mats):
    n = len(mats)
    lane = lax.broadcasted_iota(jnp.int32, (8, 128), 1)
    sub = lax.broadcasted_iota(jnp.int32, (8, 128), 0)
    mats = [[a[8 * i:8 * i + 8] for i in range(16)] for a in mats]
    for g in range(16):
        for t in range(n):
            a = mats[t]
            base = 8 * g
            a0 = a[g]
            qs, inside = pivots(a0, base, lane, sub)
            h, m, l = split3(a0)
            lhs = jnp.concatenate([h, h, m, h, l, m], axis=0).astype(jnp.bfloat16)
            h, m, l = split3(qs)
            rhs = jnp.concatenate([h, m, h, l, h, m], axis=0).astype(jnp.bfloat16)
            upd = lax.dot_general(lhs, rhs, (((0,), (0,)), ((), ())), preferred_element_type=jnp.float32)
            new = []
            for i in range(16):
                if i == g:
                    v = qs
                elif i == g + 1:
                    v = jnp.where(inside, 0.0, a[i])
                    t1 = v - lanes(a[i], base) * subl(qs, 0)
                    t2 = lanes(a[i], base + 1) * subl(qs, 1)
                    for m in range(2, 8, 2):
                        t1 = t1 - lanes(a[i], base + m) * subl(qs, m)
                        t2 = t2 + lanes(a[i], base + m + 1) * subl(qs, m + 1)
                    v = t1 - t2
                else:
                    v = jnp.where(inside, 0.0, a[i]) - upd[8 * i:8 * i + 8]
                new.append(v)
            mats[t] = new
        yield None
    yield [-jnp.concatenate(a, axis=0) for a in mats]


def dot(a, b, ca=1, cb=0):
    return lax.dot_general(a, b, (((ca,), (cb,)), ((), ())), precision=HI, preferred_element_type=jnp.float32)


MESH = pl.DeviceIdType.MESH
FOLDS = 5
BLOCK = 512
TRAITS = 8
CHUNKS = [[0, 1], [2, 3], [4, 5], [6, 7], [8], [9]]
XY_CHUNK = 1
FIRST = 4
STEPS = len(CHUNKS)
ROWS = [16 * len(c) + (8 if i == XY_CHUNK else 0) for i, c in enumerate(CHUNKS)]
START = [sum(ROWS[:i]) for i in range(STEPS)]
TOTAL = sum(ROWS)
PLACE = {slot: START[i] + 16 * n for i, c in enumerate(CHUNKS) for n, slot in enumerate(c)}
XY_PLACE = START[XY_CHUNK] + 16 * len(CHUNKS[XY_CHUNK])


def fit_kernel(lam_ref, x_ref, yt_ref, fold_ref, beta_ref, out_ref, s_ref, t_ref, y_ref, b_ref, xv, lhs, part, relay, plain, comb, half, zin, done,
                load, send, recv, gsend, grecv):
    me = lax.axis_index("smp")
    y, z = lax.div(me, 2), lax.rem(me, 2)
    right = lax.rem(y + 1, 4) * 2 + z
    left = lax.rem(y + 3, 4) * 2 + z
    across = lax.rem(y + 2, 4)
    other = y * 2 + (1 - z)
    barrier = pltpu.get_barrier_semaphore()
    loads = [pltpu.make_async_copy(x_ref.at[:, pl.ds(128 * p, 128)], xv.at[:, pl.ds(128 * p, 128)], load.at[p])
             for p in range(NB)]
    for c in loads:
        c.start()
    for i in range(1, 8):
        pl.semaphore_signal(barrier, inc=1, device_id={"smp": lax.rem(me + i, 8)}, device_id_type=MESH)

    @pl.when(me >= FOLDS)
    def _():
        out_ref[...] = jnp.zeros_like(out_ref)

    masks = [jnp.where(fold_ref[...] != k, 1.0, 0.0).astype(jnp.bfloat16) for k in range(FOLDS)]
    ready = set()

    def span(c):
        return pl.ds(FOLDS * START[c], FOLDS * ROWS[c])

    def hop(kind, c, src, dst, device):
        return pltpu.make_async_remote_copy(
            src_ref=src, dst_ref=dst, send_sem=send.at[kind, c], recv_sem=recv.at[kind, c],
            device_id={"smp": device}, device_id_type=MESH)

    def relays(c):
        return [hop(0, c, part.at[across * 2, span(c)], relay.at[0, span(c)], right),
                hop(1, c, part.at[across * 2 + 1, span(c)], relay.at[1, span(c)], left)]

    def plains(c):
        return [hop(2, c, part.at[lax.rem(y + 1, 4) * 2 + 1, span(c)], plain.at[0, span(c)], right),
                hop(3, c, part.at[lax.rem(y + 3, 4) * 2, span(c)], plain.at[1, span(c)], left)]

    def combs(c):
        return [hop(4, c, relay.at[0, span(c)], comb.at[0, span(c)], right),
                hop(5, c, relay.at[1, span(c)], comb.at[1, span(c)], left)]

    def cross_z(c):
        return hop(6, c, half.at[span(c)], zin.at[span(c)], other)

    def gather(c, k, sender):
        return pltpu.make_async_remote_copy(
            src_ref=done.at[pl.ds(FOLDS * START[c] + k * ROWS[c], ROWS[c])],
            dst_ref=out_ref.at[sender, pl.ds(START[c], ROWS[c])],
            send_sem=gsend.at[c, k], recv_sem=grecv.at[c, sender], device_id={"smp": k}, device_id_type=MESH)

    def rows_of(p):
        if p in ready:
            return
        ready.add(p)
        loads[p].wait()
        xt = jnp.transpose(xv[:, 128 * p:128 * p + 128])
        for k in range(FOLDS):
            lhs[p, 128 * k:128 * k + 128, :] = xt * masks[k]

    def products(c):
        slots = CHUNKS[c]
        p, q = BLK[slots[0]]
        wide = len(slots) == 2 and BLK[slots[1]] == (p, q + 1)
        for n, slot in enumerate(slots):
            p, q = BLK[slot]
            rows_of(p)
            if q not in ready:
                rows_of(q)
            if wide and n == 0:
                rows_of(q + 1)
                both = jnp.dot(lhs[p], xv[:, 128 * q:128 * q + 256], preferred_element_type=jnp.float32)
            v = both[:, 128 * n:128 * n + 128] if wide else jnp.dot(
                lhs[p], xv[:, 128 * q:128 * q + 128], preferred_element_type=jnp.float32)
            for k in range(FOLDS):
                for s in range(8):
                    r = FOLDS * START[c] + k * ROWS[c] + 16 * n
                    part[s, r:r + 16, :] = v[128 * k + 16 * s:128 * k + 16 * s + 16, :]
        if c == XY_CHUNK:
            for p in range(NB):
                rows_of(p)
            yt = yt_ref[...]
            v = jnp.dot(jnp.concatenate([yt * m for m in masks], axis=0), xv[...], preferred_element_type=jnp.float32)
            for k in range(FOLDS):
                r = FOLDS * START[c] + (k + 1) * ROWS[c] - 8
                for s in range(8):
                    for q in range(NB):
                        part[s, r + q:r + q + 1, :] = v[16 * k + s:16 * k + s + 1, 128 * q:128 * q + 128]
                    part[s, r + 4:r + 8, :] = jnp.zeros((4, 128), jnp.float32)

    def arrived(g):
        @pl.when(me < FOLDS)
        def _():
            def one(i, carry):
                gather(g, 0, lax.rem(me + i, 8)).wait_recv()
                return carry

            lax.fori_loop(1, 8, one, 0)

        row = lax.broadcasted_iota(jnp.int32, (128, 128), 0)
        col = lax.broadcasted_iota(jnp.int32, (128, 128), 1)
        for slot in CHUNKS[g]:
            p, q = BLK[slot]
            r = PLACE[slot]
            v = jnp.concatenate([out_ref[s, r:r + 16, :] for s in range(8)], axis=0)
            for j in range(2):
                w = v if p < q else v + jnp.where(row == col, lam_ref[j] * float(8 * x_ref.shape[0]), 0.0)
                s_ref[j, p, :, 128 * q:128 * q + 128] = w
        if g == XY_CHUNK:
            for s in range(8):
                for q in range(NB):
                    for j in range(2):
                        y_ref[j, s:s + 1, 128 * q:128 * q + 128] = out_ref[s, XY_PLACE + q:XY_PLACE + q + 1, :]

    def subtract(p, q):
        for j in range(2):
            a = s_ref[j, p, :, 128 * q:128 * q + 128]
            s_ref[j, q, :, 128 * q:] = s_ref[j, q, :, 128 * q:] - dot(a, t_ref[j, p, :, 128 * q:], 0, 0)

    def tasks():
        arrived(0)
        for p in range(NB):
            lo, hi = 128 * p, 128 * p + 128
            for n, ws in enumerate(inverse([s_ref[j, p, :, lo:hi] for j in range(2)])):
                if n % 8 == 7:
                    yield None
            if p == 0:
                arrived(1)
            for j in range(2):
                y = dot(y_ref[j, :, lo:hi], ws[j])
                y_ref[j, :, lo:hi] = y
                if p + 1 < NB:
                    right = s_ref[j, p, :, hi:]
                    t_ref[j, p, :, hi:] = dot(ws[j], right)
                    y_ref[j, :, hi:] = y_ref[j, :, hi:] - dot(y, right)
            if p == 0:
                yield None
                arrived(2)
                arrived(3)
                subtract(0, 1)
                yield None
            elif p == 1:
                arrived(4)
                arrived(5)
                for q in range(2, NB):
                    subtract(0, q)
                    subtract(1, q)
            elif p == 2:
                subtract(2, 3)
        for p in range(NB - 2, -1, -1):
            lo, hi = 128 * p, 128 * p + 128
            for j in range(2):
                y_ref[j, :, lo:hi] = y_ref[j, :, lo:hi] - dot(y_ref[j, :, hi:], t_ref[j, p, :, hi:], 1, 1)
        for t in range(TRAITS):
            for j in range(2):
                b_ref[2 * t + j:2 * t + j + 1, :] = y_ref[j, t:t + 1, :]
        beta_ref[...] = b_ref[...].astype(jnp.bfloat16)

    solving = tasks()

    for i in range(STEPS + 3):
        if i < STEPS:
            products(i)
            if i == 0:
                pl.semaphore_wait(barrier, 7)
            for c in relays(i) + plains(i):
                c.start()
        if 1 <= i <= STEPS:
            g = i - 1
            for c in relays(g):
                c.wait_recv()
            relay[0, span(g)] += part[lax.rem(y + 1, 4) * 2, span(g)]
            relay[1, span(g)] += part[lax.rem(y + 3, 4) * 2 + 1, span(g)]
            for c in combs(g):
                c.start()
        if 2 <= i <= STEPS + 1:
            g = i - 2
            for c in plains(g) + combs(g):
                c.wait_recv()
            zero = part[y * 2, span(g)] + plain[1, span(g)] + comb[0, span(g)]
            one = part[y * 2 + 1, span(g)] + plain[0, span(g)] + comb[1, span(g)]
            half[span(g)] = jnp.where(z == 0, one, zero)
            done[span(g)] = jnp.where(z == 0, zero, one)
            cross_z(g).start()
        if i >= 3:
            g = i - 3
            cross_z(g).wait_recv()
            done[span(g)] += zin[span(g)]
            for k in range(FOLDS):
                @pl.when(me != k)
                def _():
                    gather(g, k, me).start()

                @pl.when(me == k)
                def _():
                    r = FOLDS * START[g] + k * ROWS[g]
                    out_ref[me, START[g]:START[g] + ROWS[g], :] = done[r:r + ROWS[g], :]
        if i >= FIRST:
            next(solving)

    for _ in solving:
        pass
    for g in range(STEPS):
        for c in relays(g) + plains(g) + combs(g) + [cross_z(g)]:
            c.wait_send()
        for k in range(FOLDS):
            @pl.when(me != k)
            def _():
                gather(g, k, me).wait_send()


def fit(lam, x, yt, fold):
    vmem = pl.BlockSpec(memory_space=pltpu.VMEM)
    f32 = jnp.float32
    rows = FOLDS * TOTAL
    return pl.pallas_call(
        fit_kernel,
        out_shape=jax.ShapeDtypeStruct((16, BLOCK), jnp.bfloat16),
        in_specs=[pl.BlockSpec(memory_space=pltpu.SMEM), pl.BlockSpec(memory_space=pltpu.HBM), vmem, vmem],
        out_specs=vmem,
        scratch_shapes=[
            pltpu.VMEM((8, TOTAL, 128), f32),
            pltpu.VMEM((2, NB, 128, BLOCK), f32),
            pltpu.VMEM((2, NB, 128, BLOCK), f32),
            pltpu.VMEM((2, TRAITS, BLOCK), f32),
            pltpu.VMEM((16, BLOCK), f32),
            pltpu.VMEM(x.shape, jnp.bfloat16),
            pltpu.VMEM((NB, 128 * FOLDS, x.shape[0]), jnp.bfloat16),
            pltpu.VMEM((8, rows, 128), f32),
            pltpu.VMEM((2, rows, 128), f32),
            pltpu.VMEM((2, rows, 128), f32),
            pltpu.VMEM((2, rows, 128), f32),
            pltpu.VMEM((rows, 128), f32),
            pltpu.VMEM((rows, 128), f32),
            pltpu.VMEM((rows, 128), f32),
            pltpu.SemaphoreType.DMA((NB,)),
            pltpu.SemaphoreType.DMA((7, STEPS)),
            pltpu.SemaphoreType.DMA((7, STEPS)),
            pltpu.SemaphoreType.DMA((STEPS, FOLDS)),
            pltpu.SemaphoreType.DMA((STEPS, 8)),
        ],
        compiler_params=pltpu.CompilerParams(collective_id=1, has_side_effects=True, vmem_limit_bytes=48 << 20),
    )(lam, x, yt, fold)


def tail_kernel(beta_ref, x_ref, fold_ref, old_ref, oof_ref, cross_ref, betas, mine, feats, terms, rows, sums,
                bsend, brecv, fsend, frecv, tsend, trecv, ssend, srecv):
    s, b = lax.axis_index("smp"), lax.axis_index("blk")
    samples = x_ref.shape[0]
    barrier = pltpu.get_barrier_semaphore()

    def greet_smp(i, carry):
        pl.semaphore_signal(barrier, inc=1, device_id={"smp": lax.rem(s + i, 8)}, device_id_type=MESH)
        return carry

    def greet_blk(i, carry):
        pl.semaphore_signal(barrier, inc=1, device_id={"blk": lax.rem(b + i, 16)}, device_id_type=MESH)
        return carry

    lax.fori_loop(1, 8, greet_smp, 0)
    lax.fori_loop(1, 16, greet_blk, 0)
    pl.semaphore_wait(barrier, 22)

    def spread(i):
        return pltpu.make_async_remote_copy(
            src_ref=beta_ref, dst_ref=betas.at[s], send_sem=bsend.at[i], recv_sem=brecv.at[s],
            device_id={"smp": lax.rem(s + i, 8)}, device_id_type=MESH)

    def start_spread(i, carry):
        spread(i).start()
        return carry

    def end_spread(i, carry):
        spread(i).wait_send()
        return carry

    @pl.when(s < FOLDS)
    def _():
        lax.fori_loop(1, 8, start_spread, 0)
        betas[s] = beta_ref[...]

    def beta_in(k, carry):
        @pl.when(s != k)
        def _():
            pltpu.make_async_remote_copy(
                src_ref=beta_ref, dst_ref=betas.at[k], send_sem=bsend.at[0], recv_sem=brecv.at[k],
                device_id={"smp": k}, device_id_type=MESH).wait_recv()
        return carry

    lax.fori_loop(0, FOLDS, beta_in, 0)
    flat = jnp.concatenate([betas[k] for k in range(FOLDS)], axis=0)
    fitted = lax.dot_general(flat, x_ref[...], (((1,), (1,)), ((), ())), preferred_element_type=jnp.float32)
    fold = fold_ref[...]
    chosen = jnp.zeros((16, samples), jnp.float32)
    for k in range(FOLDS):
        chosen = jnp.where(fold == k, fitted[16 * k:16 * k + 16, :], chosen)
    oof = (chosen * math.sqrt(8 * samples / BLOCK)).astype(jnp.bfloat16)
    oof_ref[...] = oof
    for c in range(16):
        mine[c] = oof[:, 128 * c:128 * c + 128]
    feats[b] = mine[b]

    def feature(i):
        to = lax.rem(b + i, 16)
        return pltpu.make_async_remote_copy(
            src_ref=mine.at[to], dst_ref=feats.at[b], send_sem=fsend.at[i], recv_sem=frecv.at[i],
            device_id={"blk": to}, device_id_type=MESH)

    def start_feature(i, carry):
        feature(i).start()
        return carry

    def end_feature(i, carry):
        feature(i).wait()
        return carry

    lax.fori_loop(1, 16, start_feature, 0)
    lax.fori_loop(1, 16, end_feature, 0)
    f = jnp.concatenate([feats[c] for c in range(16)], axis=0)
    nt = (((1,), (1,)), ((), ()))
    against_old = lax.dot_general(f, old_ref[...], nt, preferred_element_type=jnp.float32)
    against_new = lax.dot_general(f, f, nt, preferred_element_type=jnp.float32)
    r = lax.broadcasted_iota(jnp.int32, (256, 256), 0)
    c = lax.broadcasted_iota(jnp.int32, (256, 256), 1)
    row_trait = (r >> 1) & 7
    against_old = jnp.where(row_trait == (c >> 5), against_old, 0.0)
    against_new = jnp.where(row_trait == ((c >> 1) & 7), against_new, 0.0)
    r = lax.broadcasted_iota(jnp.int32, (256, 128), 0)
    c = lax.broadcasted_iota(jnp.int32, (256, 128), 1)
    pick_old = jnp.where((r & 31) == c, 1.0, 0.0)
    pick_new = jnp.where(32 + ((r >> 4) << 1) + (r & 1) == c, 1.0, 0.0)
    total = dot(against_old, pick_old) + dot(against_new, pick_new)
    for k in range(16):
        terms[k] = total[16 * k:16 * k + 16, :]
    rows[b] = terms[b]

    def term(i):
        to = lax.rem(b + i, 16)
        return pltpu.make_async_remote_copy(
            src_ref=terms.at[to], dst_ref=rows.at[b], send_sem=tsend.at[i], recv_sem=trecv.at[i],
            device_id={"blk": to}, device_id_type=MESH)

    def start_term(i, carry):
        term(i).start()
        return carry

    def end_term(i, carry):
        term(i).wait()
        return carry

    lax.fori_loop(1, 16, start_term, 0)
    lax.fori_loop(1, 16, end_term, 0)
    part = rows[0]
    for k in range(1, 16):
        part = part + rows[k]
    sums[s] = part

    def last(i):
        return pltpu.make_async_remote_copy(
            src_ref=sums.at[s], dst_ref=sums.at[s], send_sem=ssend.at[i], recv_sem=srecv.at[i],
            device_id={"smp": lax.rem(s + i, 8)}, device_id_type=MESH)

    def start_last(i, carry):
        last(i).start()
        return carry

    def end_last(i, carry):
        last(i).wait()
        return carry

    lax.fori_loop(1, 8, start_last, 0)
    lax.fori_loop(1, 8, end_last, 0)
    final = sums[0]
    for k in range(1, 8):
        final = final + sums[k]
    cross_ref[...] = final * (1.0 / (8 * samples))

    @pl.when(s < FOLDS)
    def _():
        lax.fori_loop(1, 8, end_spread, 0)


def tail(beta, x, fold, old):
    vmem = pl.BlockSpec(memory_space=pltpu.VMEM)
    dma = pltpu.SemaphoreType.DMA
    return pl.pallas_call(
        tail_kernel,
        out_shape=(jax.ShapeDtypeStruct((16, x.shape[0]), jnp.bfloat16), jax.ShapeDtypeStruct((16, 128), jnp.float32)),
        in_specs=[vmem] * 4,
        out_specs=(vmem, vmem),
        scratch_shapes=[
            pltpu.VMEM((FOLDS, 16, BLOCK), jnp.bfloat16),
            pltpu.VMEM((16, 16, 128), jnp.bfloat16),
            pltpu.VMEM((16, 16, 128), jnp.bfloat16),
            pltpu.VMEM((16, 16, 128), jnp.float32),
            pltpu.VMEM((16, 16, 128), jnp.float32),
            pltpu.VMEM((8, 16, 128), jnp.float32),
            dma((8,)), dma((8,)), dma((16,)), dma((16,)), dma((16,)), dma((16,)), dma((8,)), dma((8,)),
        ],
        compiler_params=pltpu.CompilerParams(collective_id=2, has_side_effects=True, vmem_limit_bytes=40 << 20),
    )(beta, x, fold, old)


def local(x, y, fold, lam, old):
    rows = x.shape[0]
    fold = fold[None, :]
    yt = jnp.pad(y.T, ((0, 8), (0, 0)))
    beta = fit(lam, x, yt, fold)
    before = jnp.transpose(old[0], (1, 2, 0)).reshape(256, 128)
    oof, cross = tail(beta, x, fold, before)
    here = lax.dynamic_slice_in_dim(cross, 8 * lax.axis_index("smp"), 8, 1)
    return jnp.transpose(oof.reshape(TRAITS, 2, rows), (2, 0, 1)), here.reshape(TRAITS, 2, 8)


def solution(mesh):
    return jax.shard_map(
        local,
        mesh=mesh,
        in_specs=(P("smp", "blk"), P("smp", None), P("smp"), P(), P("smp", "blk", None, None)),
        out_specs=(P("smp", None, "blk"), P(None, "blk", "smp")),
        check_vma=False,
    )
```

```python
import math

import jax
import jax.numpy as jnp
from jax import lax
from jax.experimental import pallas as pl
from jax.experimental.pallas import tpu as pltpu
from jax.sharding import PartitionSpec as P

HI = lax.Precision.HIGHEST
NB = 4
BLK = [(p, q) for p in range(NB) for q in range(p, NB)]
IDX = {pq: i for i, pq in enumerate(BLK)}


def lanes(x, m):
    return jnp.broadcast_to(x[:, m:m + 1], x.shape)


def subl(x, m):
    return jnp.broadcast_to(x[m:m + 1, :], x.shape)


def split3(x):
    hi = x.astype(jnp.bfloat16).astype(jnp.float32)
    r = x - hi
    mid = r.astype(jnp.bfloat16).astype(jnp.float32)
    return hi, mid, r - mid


def pivots(a0, base, lane, sub):
    cols = [lanes(a0, base + m) for m in range(8)]
    inside = (lane >= base) & (lane < base + 8)
    z = jnp.where(inside, jnp.where(lane - base == sub, -1.0, 0.0), a0)
    scale = None
    for m in range(8):
        d = 1.0 / subl(cols[m], m)
        l = jnp.where(sub == m, 0.0, cols[m] * d)
        z = z - l * subl(z, m)
        for j in range(m + 1, 8):
            cols[j] = cols[j] - l * subl(cols[j], m)
        scale = d if m == 0 else jnp.where(sub == m, d, scale)
    return z * scale, inside


def inverse(mats):
    n = len(mats)
    lane = lax.broadcasted_iota(jnp.int32, (8, 128), 1)
    sub = lax.broadcasted_iota(jnp.int32, (8, 128), 0)
    mats = [[a[8 * i:8 * i + 8] for i in range(16)] for a in mats]
    for g in range(16):
        for t in range(n):
            a = mats[t]
            base = 8 * g
            a0 = a[g]
            qs, inside = pivots(a0, base, lane, sub)
            h, m, l = split3(a0)
            lhs = jnp.concatenate([h, h, m, h, l, m], axis=0).astype(jnp.bfloat16)
            h, m, l = split3(qs)
            rhs = jnp.concatenate([h, m, h, l, h, m], axis=0).astype(jnp.bfloat16)
            upd = lax.dot_general(lhs, rhs, (((0,), (0,)), ((), ())), preferred_element_type=jnp.float32)
            new = []
            for i in range(16):
                if i == g:
                    v = qs
                elif i == g + 1:
                    v = jnp.where(inside, 0.0, a[i])
                    t1 = v - lanes(a[i], base) * subl(qs, 0)
                    t2 = lanes(a[i], base + 1) * subl(qs, 1)
                    for m in range(2, 8, 2):
                        t1 = t1 - lanes(a[i], base + m) * subl(qs, m)
                        t2 = t2 + lanes(a[i], base + m + 1) * subl(qs, m + 1)
                    v = t1 - t2
                else:
                    v = jnp.where(inside, 0.0, a[i]) - upd[8 * i:8 * i + 8]
                new.append(v)
            mats[t] = new
        yield None
    yield [-jnp.concatenate(a, axis=0) for a in mats]


def dot(a, b, ca=1, cb=0):
    return lax.dot_general(a, b, (((ca,), (cb,)), ((), ())), precision=HI, preferred_element_type=jnp.float32)


MESH = pl.DeviceIdType.MESH
FOLDS = 5
BLOCK = 512
TRAITS = 8
CHUNKS = [[0, 1], [2, 3], [4, 5], [6, 7], [8], [9]]
XY_CHUNK = 1
FIRST = 4
STEPS = len(CHUNKS)
ROWS = [16 * len(c) + (8 if i == XY_CHUNK else 0) for i, c in enumerate(CHUNKS)]
START = [sum(ROWS[:i]) for i in range(STEPS)]
TOTAL = sum(ROWS)
PLACE = {slot: START[i] + 16 * n for i, c in enumerate(CHUNKS) for n, slot in enumerate(c)}
XY_PLACE = START[XY_CHUNK] + 16 * len(CHUNKS[XY_CHUNK])


def fit_kernel(lam_ref, x_ref, yt_ref, fold_ref, beta_ref, out_ref, s_ref, t_ref, y_ref, b_ref, xv, lhs, part, relay, plain, comb, half, zin, done,
                load, send, recv, gsend, grecv):
    me = lax.axis_index("smp")
    fold_here = lax.rem(3 * me, 8)
    y, z = lax.div(me, 2), lax.rem(me, 2)
    right = lax.rem(y + 1, 4) * 2 + z
    left = lax.rem(y + 3, 4) * 2 + z
    across = lax.rem(y + 2, 4)
    other = y * 2 + (1 - z)
    barrier = pltpu.get_barrier_semaphore()
    loads = [pltpu.make_async_copy(x_ref.at[:, pl.ds(128 * p, 128)], xv.at[:, pl.ds(128 * p, 128)], load.at[p])
             for p in range(NB)]
    for c in loads:
        c.start()
    for i in range(1, 8):
        pl.semaphore_signal(barrier, inc=1, device_id={"smp": lax.rem(me + i, 8)}, device_id_type=MESH)

    @pl.when(fold_here >= FOLDS)
    def _():
        out_ref[...] = jnp.zeros_like(out_ref)

    y_rows = jnp.concatenate([yt_ref[...].astype(jnp.float32), jnp.zeros((8, x_ref.shape[0]), jnp.float32)], axis=0)
    y_rows = y_rows.astype(jnp.bfloat16)
    masks = [jnp.where(fold_ref[...] != k, 1.0, 0.0).astype(jnp.bfloat16) for k in range(FOLDS)]
    ready = set()

    def span(c):
        return pl.ds(FOLDS * START[c], FOLDS * ROWS[c])

    def hop(kind, c, src, dst, device):
        return pltpu.make_async_remote_copy(
            src_ref=src, dst_ref=dst, send_sem=send.at[kind, c], recv_sem=recv.at[kind, c],
            device_id={"smp": device}, device_id_type=MESH)

    def relays(c):
        return [hop(0, c, part.at[across * 2, span(c)], relay.at[0, span(c)], right),
                hop(1, c, part.at[across * 2 + 1, span(c)], relay.at[1, span(c)], left)]

    def plains(c):
        return [hop(2, c, part.at[lax.rem(y + 1, 4) * 2 + 1, span(c)], plain.at[0, span(c)], right),
                hop(3, c, part.at[lax.rem(y + 3, 4) * 2, span(c)], plain.at[1, span(c)], left)]

    def combs(c):
        return [hop(4, c, relay.at[0, span(c)], comb.at[0, span(c)], right),
                hop(5, c, relay.at[1, span(c)], comb.at[1, span(c)], left)]

    def cross_z(c):
        return hop(6, c, half.at[span(c)], zin.at[span(c)], other)

    def gather(c, k, sender):
        return pltpu.make_async_remote_copy(
            src_ref=done.at[pl.ds(FOLDS * START[c] + k * ROWS[c], ROWS[c])],
            dst_ref=out_ref.at[sender, pl.ds(START[c], ROWS[c])],
            send_sem=gsend.at[c, k], recv_sem=grecv.at[c, sender], device_id={"smp": 3 * k % 8}, device_id_type=MESH)

    def rows_of(p):
        if p in ready:
            return
        ready.add(p)
        loads[p].wait()
        xt = jnp.transpose(xv[:, 128 * p:128 * p + 128])
        for k in range(FOLDS):
            lhs[p, 128 * k:128 * k + 128, :] = xt * masks[k]

    def products(c):
        slots = CHUNKS[c]
        p, q = BLK[slots[0]]
        wide = len(slots) == 2 and BLK[slots[1]] == (p, q + 1)
        for n, slot in enumerate(slots):
            p, q = BLK[slot]
            rows_of(p)
            if q not in ready:
                rows_of(q)
            if wide and n == 0:
                rows_of(q + 1)
                both = jnp.dot(lhs[p], xv[:, 128 * q:128 * q + 256], preferred_element_type=jnp.float32)
            v = both[:, 128 * n:128 * n + 128] if wide else jnp.dot(
                lhs[p], xv[:, 128 * q:128 * q + 128], preferred_element_type=jnp.float32)
            for k in range(FOLDS):
                for s in range(8):
                    r = FOLDS * START[c] + k * ROWS[c] + 16 * n
                    part[s, r:r + 16, :] = v[128 * k + 16 * s:128 * k + 16 * s + 16, :]
        if c == XY_CHUNK:
            for p in range(NB):
                rows_of(p)
            v = jnp.dot(jnp.concatenate([y_rows * m for m in masks], axis=0), xv[...], preferred_element_type=jnp.float32)
            for k in range(FOLDS):
                r = FOLDS * START[c] + (k + 1) * ROWS[c] - 8
                for s in range(8):
                    for q in range(NB):
                        part[s, r + q:r + q + 1, :] = v[16 * k + s:16 * k + s + 1, 128 * q:128 * q + 128]
                    part[s, r + 4:r + 8, :] = jnp.zeros((4, 128), jnp.float32)

    def arrived(g):
        @pl.when(fold_here < FOLDS)
        def _():
            def one(i, carry):
                gather(g, 0, lax.rem(me + i, 8)).wait_recv()
                return carry

            lax.fori_loop(1, 8, one, 0)

        row = lax.broadcasted_iota(jnp.int32, (128, 128), 0)
        col = lax.broadcasted_iota(jnp.int32, (128, 128), 1)
        for slot in CHUNKS[g]:
            p, q = BLK[slot]
            r = PLACE[slot]
            v = jnp.concatenate([out_ref[s, r:r + 16, :] for s in range(8)], axis=0)
            for j in range(2):
                w = v if p < q else v + jnp.where(row == col, lam_ref[j] * float(8 * x_ref.shape[0]), 0.0)
                s_ref[j, p, :, 128 * q:128 * q + 128] = w
        if g == XY_CHUNK:
            for s in range(8):
                for q in range(NB):
                    for j in range(2):
                        y_ref[j, s:s + 1, 128 * q:128 * q + 128] = out_ref[s, XY_PLACE + q:XY_PLACE + q + 1, :]

    def subtract(p, q, first, last):
        cols = slice(128 * first, 128 * last)
        for j in range(2):
            a = s_ref[j, p, :, 128 * q:128 * q + 128]
            s_ref[j, q, :, cols] = s_ref[j, q, :, cols] - dot(a, t_ref[j, p, :, cols], 0, 0)

    def eliminate(p, ws):
        lo, hi = 128 * p, 128 * p + 128
        for j in range(2):
            y = dot(y_ref[j, :, lo:hi], ws[j])
            y_ref[j, :, lo:hi] = y
            if p + 1 < NB:
                right = s_ref[j, p, :, hi:]
                t_ref[j, p, :, hi:] = dot(ws[j], right)
                y_ref[j, :, hi:] = y_ref[j, :, hi:] - dot(y, right)

    def diagonal(p):
        return inverse([s_ref[j, p, :, 128 * p:128 * p + 128] for j in range(2)])

    def tasks():
        arrived(0)
        for n, ws in enumerate(diagonal(0)):
            if n == 7:
                yield None
        arrived(1)
        eliminate(0, ws)
        yield None
        arrived(2)
        subtract(0, 1, 1, 3)
        for n, ws in enumerate(diagonal(1)):
            if n in (7, 15):
                yield None
        arrived(3)
        subtract(0, 1, 3, 4)
        eliminate(1, ws)
        subtract(0, 2, 2, 3)
        subtract(1, 2, 2, 3)
        for n, ws in enumerate(diagonal(2)):
            if n == 7:
                yield None
        arrived(4)
        subtract(0, 2, 3, 4)
        subtract(1, 2, 3, 4)
        eliminate(2, ws)
        arrived(5)
        for q in range(3):
            subtract(q, 3, 3, 4)
        for n, ws in enumerate(diagonal(3)):
            pass
        eliminate(3, ws)
        for p in range(NB - 2, -1, -1):
            lo, hi = 128 * p, 128 * p + 128
            for j in range(2):
                y_ref[j, :, lo:hi] = y_ref[j, :, lo:hi] - dot(y_ref[j, :, hi:], t_ref[j, p, :, hi:], 1, 1)
        for t in range(TRAITS):
            for j in range(2):
                b_ref[2 * t + j:2 * t + j + 1, :] = y_ref[j, t:t + 1, :]
        beta_ref[...] = b_ref[...].astype(jnp.bfloat16)

    solving = tasks()

    for i in range(STEPS + 3):
        if i < STEPS:
            products(i)
            if i == 0:
                pl.semaphore_wait(barrier, 7)
            for c in relays(i) + plains(i):
                c.start()
        if 1 <= i <= STEPS:
            g = i - 1
            for c in relays(g):
                c.wait_recv()
            relay[0, span(g)] += part[lax.rem(y + 1, 4) * 2, span(g)]
            relay[1, span(g)] += part[lax.rem(y + 3, 4) * 2 + 1, span(g)]
            for c in combs(g):
                c.start()
        if 2 <= i <= STEPS + 1:
            g = i - 2
            for c in plains(g) + combs(g):
                c.wait_recv()
            zero = part[y * 2, span(g)] + plain[1, span(g)] + comb[0, span(g)]
            one = part[y * 2 + 1, span(g)] + plain[0, span(g)] + comb[1, span(g)]
            half[span(g)] = jnp.where(z == 0, one, zero)
            done[span(g)] = jnp.where(z == 0, zero, one)
            cross_z(g).start()
        if i >= 3:
            g = i - 3
            cross_z(g).wait_recv()
            done[span(g)] += zin[span(g)]
            for k in range(FOLDS):
                @pl.when(fold_here != k)
                def _():
                    gather(g, k, me).start()

                @pl.when(fold_here == k)
                def _():
                    r = FOLDS * START[g] + k * ROWS[g]
                    out_ref[me, START[g]:START[g] + ROWS[g], :] = done[r:r + ROWS[g], :]
        if i >= FIRST:
            next(solving)

    for _ in solving:
        pass
    for g in range(STEPS):
        for c in relays(g) + plains(g) + combs(g) + [cross_z(g)]:
            c.wait_send()
        for k in range(FOLDS):
            @pl.when(fold_here != k)
            def _():
                gather(g, k, me).wait_send()


def fit(lam, x, yt, fold):
    vmem = pl.BlockSpec(memory_space=pltpu.VMEM)
    f32 = jnp.float32
    rows = FOLDS * TOTAL
    return pl.pallas_call(
        fit_kernel,
        out_shape=jax.ShapeDtypeStruct((16, BLOCK), jnp.bfloat16),
        in_specs=[pl.BlockSpec(memory_space=pltpu.SMEM), pl.BlockSpec(memory_space=pltpu.HBM), vmem, vmem],
        out_specs=vmem,
        scratch_shapes=[
            pltpu.VMEM((8, TOTAL, 128), f32),
            pltpu.VMEM((2, NB, 128, BLOCK), f32),
            pltpu.VMEM((2, NB, 128, BLOCK), f32),
            pltpu.VMEM((2, TRAITS, BLOCK), f32),
            pltpu.VMEM((16, BLOCK), f32),
            pltpu.VMEM(x.shape, jnp.bfloat16),
            pltpu.VMEM((NB, 128 * FOLDS, x.shape[0]), jnp.bfloat16),
            pltpu.VMEM((8, rows, 128), f32),
            pltpu.VMEM((2, rows, 128), f32),
            pltpu.VMEM((2, rows, 128), f32),
            pltpu.VMEM((2, rows, 128), f32),
            pltpu.VMEM((rows, 128), f32),
            pltpu.VMEM((rows, 128), f32),
            pltpu.VMEM((rows, 128), f32),
            pltpu.SemaphoreType.DMA((NB,)),
            pltpu.SemaphoreType.DMA((7, STEPS)),
            pltpu.SemaphoreType.DMA((7, STEPS)),
            pltpu.SemaphoreType.DMA((STEPS, FOLDS)),
            pltpu.SemaphoreType.DMA((STEPS, 8)),
        ],
        compiler_params=pltpu.CompilerParams(collective_id=1, has_side_effects=True, vmem_limit_bytes=62 << 20),
    )(lam, x, yt, fold)


def tail_kernel(beta_ref, x_ref, fold_ref, old_ref, oof_ref, cross_ref, xv, betas, mine, feats, terms, rows, sums,
                load, bsend, brecv, fsend, frecv, tsend, trecv, ssend, srecv):
    s, b = lax.axis_index("smp"), lax.axis_index("blk")
    fold_here = lax.rem(3 * s, 8)
    samples = x_ref.shape[0]
    fetch = pltpu.make_async_copy(x_ref, xv, load.at[0])
    fetch.start()
    barrier = pltpu.get_barrier_semaphore()

    def greet_smp(i, carry):
        pl.semaphore_signal(barrier, inc=1, device_id={"smp": lax.rem(s + i, 8)}, device_id_type=MESH)
        return carry

    def greet_blk(i, carry):
        pl.semaphore_signal(barrier, inc=1, device_id={"blk": lax.rem(b + i, 16)}, device_id_type=MESH)
        return carry

    for i in range(1, 8):
        greet_smp(i, 0)
    for i in range(1, 16):
        greet_blk(i, 0)
    pl.semaphore_wait(barrier, 22)
    fetch.wait()

    def spread(i):
        return pltpu.make_async_remote_copy(
            src_ref=beta_ref, dst_ref=betas.at[fold_here], send_sem=bsend.at[i], recv_sem=brecv.at[fold_here],
            device_id={"smp": lax.rem(s + i, 8)}, device_id_type=MESH)

    def start_spread(i, carry):
        spread(i).start()
        return carry

    def end_spread(i, carry):
        spread(i).wait_send()
        return carry

    @pl.when(fold_here < FOLDS)
    def _():
        for i in range(1, 8):
            start_spread(i, 0)
        betas[fold_here] = beta_ref[...]

    def beta_in(k, carry):
        @pl.when(fold_here != k)
        def _():
            pltpu.make_async_remote_copy(
                src_ref=beta_ref, dst_ref=betas.at[k], send_sem=bsend.at[0], recv_sem=brecv.at[k],
                device_id={"smp": lax.rem(s + 1, 8)}, device_id_type=MESH).wait_recv()
        return carry

    for k in range(FOLDS):
        beta_in(k, 0)
    flat = jnp.concatenate([betas[k] for k in range(FOLDS)], axis=0)
    fitted = lax.dot_general(flat, xv[...], (((1,), (1,)), ((), ())), preferred_element_type=jnp.float32)
    fold = fold_ref[...]
    chosen = jnp.zeros((16, samples), jnp.float32)
    for k in range(FOLDS):
        chosen = jnp.where(fold == k, fitted[16 * k:16 * k + 16, :], chosen)
    oof = (chosen * math.sqrt(8 * samples / BLOCK)).astype(jnp.bfloat16)
    oof_ref[...] = oof
    for c in range(16):
        mine[c] = oof[:, 128 * c:128 * c + 128]
    feats[b] = mine[b]

    def feature(i):
        to = lax.rem(b + i, 16)
        return pltpu.make_async_remote_copy(
            src_ref=mine.at[to], dst_ref=feats.at[b], send_sem=fsend.at[i], recv_sem=frecv.at[i],
            device_id={"blk": to}, device_id_type=MESH)

    def start_feature(i, carry):
        feature(i).start()
        return carry

    def end_feature(i, carry):
        feature(i).wait()
        return carry

    for i in range(1, 16):
        start_feature(i, 0)
    r = lax.broadcasted_iota(jnp.int32, (256, 512), 0)
    c = lax.broadcasted_iota(jnp.int32, (256, 512), 1)
    same = ((r >> 1) & 7) == jnp.where(c < 256, c >> 5, (c >> 1) & 7)
    r = lax.broadcasted_iota(jnp.int32, (512, 128), 0)
    c = lax.broadcasted_iota(jnp.int32, (512, 128), 1)
    place = jnp.where(r < 256, r & 31, 32 + (((r - 256) >> 4) << 1) + (r & 1))
    pick = jnp.where(place == c, 1.0, 0.0).astype(jnp.bfloat16)
    for i in range(1, 16):
        end_feature(i, 0)
    f = jnp.concatenate([feats[c] for c in range(16)], axis=0)
    nt = (((1,), (1,)), ((), ()))
    against = lax.dot_general(f, jnp.concatenate([old_ref[...], f], axis=0), nt, preferred_element_type=jnp.float32)
    chosen = jnp.where(same, against, 0.0)
    hi = chosen.astype(jnp.bfloat16)
    rest = chosen - hi.astype(jnp.float32)
    mid = rest.astype(jnp.bfloat16)
    low = (rest - mid.astype(jnp.float32)).astype(jnp.bfloat16)
    total = jnp.dot(hi, pick, preferred_element_type=jnp.float32)
    total += jnp.dot(mid, pick, preferred_element_type=jnp.float32)
    total += jnp.dot(low, pick, preferred_element_type=jnp.float32)
    for k in range(16):
        terms[k] = total[16 * k:16 * k + 16, :]
    rows[b] = terms[b]

    def term(i):
        to = lax.rem(b + i, 16)
        return pltpu.make_async_remote_copy(
            src_ref=terms.at[to], dst_ref=rows.at[b], send_sem=tsend.at[i], recv_sem=trecv.at[i],
            device_id={"blk": to}, device_id_type=MESH)

    def start_term(i, carry):
        term(i).start()
        return carry

    def end_term(i, carry):
        term(i).wait()
        return carry

    for i in range(1, 16):
        start_term(i, 0)
    for i in range(1, 16):
        end_term(i, 0)
    part = rows[0]
    for k in range(1, 16):
        part = part + rows[k]
    sums[s] = part

    def last(i):
        return pltpu.make_async_remote_copy(
            src_ref=sums.at[s], dst_ref=sums.at[s], send_sem=ssend.at[i], recv_sem=srecv.at[i],
            device_id={"smp": lax.rem(s + i, 8)}, device_id_type=MESH)

    def start_last(i, carry):
        last(i).start()
        return carry

    def end_last(i, carry):
        last(i).wait()
        return carry

    for i in range(1, 8):
        start_last(i, 0)
    for i in range(1, 8):
        end_last(i, 0)
    final = sums[0]
    for k in range(1, 8):
        final = final + sums[k]
    cross_ref[...] = final * (1.0 / (8 * samples))

    @pl.when(fold_here < FOLDS)
    def _():
        for i in range(1, 8):
            end_spread(i, 0)


def tail(beta, x, fold, old):
    vmem = pl.BlockSpec(memory_space=pltpu.VMEM)
    dma = pltpu.SemaphoreType.DMA
    return pl.pallas_call(
        tail_kernel,
        out_shape=(jax.ShapeDtypeStruct((16, x.shape[0]), jnp.bfloat16), jax.ShapeDtypeStruct((16, 128), jnp.float32)),
        in_specs=[vmem, pl.BlockSpec(memory_space=pltpu.HBM), vmem, vmem],
        out_specs=(vmem, vmem),
        scratch_shapes=[
            pltpu.VMEM(x.shape, jnp.bfloat16),
            pltpu.VMEM((FOLDS, 16, BLOCK), jnp.bfloat16),
            pltpu.VMEM((16, 16, 128), jnp.bfloat16),
            pltpu.VMEM((16, 16, 128), jnp.bfloat16),
            pltpu.VMEM((16, 16, 128), jnp.float32),
            pltpu.VMEM((16, 16, 128), jnp.float32),
            pltpu.VMEM((8, 16, 128), jnp.float32),
            dma((1,)), dma((8,)), dma((8,)), dma((16,)), dma((16,)), dma((16,)), dma((16,)), dma((8,)), dma((8,)),
        ],
        compiler_params=pltpu.CompilerParams(collective_id=2, has_side_effects=True, vmem_limit_bytes=62 << 20),
    )(beta, x, fold, old)


def local(x, y, fold, lam, old):
    rows = x.shape[0]
    fold = fold[None, :]
    beta = fit(lam, x, y.T, fold)
    before = jnp.transpose(old[0], (1, 2, 0)).reshape(256, 128)
    oof, cross = tail(beta, x, fold, before)
    here = lax.dynamic_slice_in_dim(cross, 8 * lax.axis_index("smp"), 8, 1)
    return jnp.transpose(oof.reshape(TRAITS, 2, rows), (2, 0, 1)), here.reshape(TRAITS, 2, 8)


def solution(mesh):
    return jax.shard_map(
        local,
        mesh=mesh,
        in_specs=(P("smp", "blk"), P("smp", None), P("smp"), P(), P("smp", "blk", None, None)),
        out_specs=(P("smp", None, "blk"), P(None, "blk", "smp")),
        check_vma=False,
    )
```

```python
import math

import jax
import jax.numpy as jnp
from jax import lax
from jax.experimental import pallas as pl
from jax.experimental.pallas import tpu as pltpu
from jax.sharding import PartitionSpec as P

HI = lax.Precision.HIGHEST
NB = 4
BLK = [(p, q) for p in range(NB) for q in range(p, NB)]
IDX = {pq: i for i, pq in enumerate(BLK)}


def lanes(x, m):
    return jnp.broadcast_to(x[:, m:m + 1], x.shape)


def subl(x, m):
    return jnp.broadcast_to(x[m:m + 1, :], x.shape)


def split3(x):
    hi = x.astype(jnp.bfloat16).astype(jnp.float32)
    r = x - hi
    mid = r.astype(jnp.bfloat16).astype(jnp.float32)
    return hi, mid, r - mid


def pivots(a0, base, lane, sub):
    cols = [lanes(a0, base + m) for m in range(8)]
    inside = (lane >= base) & (lane < base + 8)
    z = jnp.where(inside, jnp.where(lane - base == sub, -1.0, 0.0), a0)
    scale = None
    for m in range(8):
        d = 1.0 / subl(cols[m], m)
        l = jnp.where(sub == m, 0.0, cols[m] * d)
        z = z - l * subl(z, m)
        for j in range(m + 1, 8):
            cols[j] = cols[j] - l * subl(cols[j], m)
        scale = d if m == 0 else jnp.where(sub == m, d, scale)
    return z * scale, inside


def inverse(mats):
    n = len(mats)
    lane = lax.broadcasted_iota(jnp.int32, (8, 128), 1)
    sub = lax.broadcasted_iota(jnp.int32, (8, 128), 0)
    mats = [[a[8 * i:8 * i + 8] for i in range(16)] for a in mats]
    for g in range(16):
        for t in range(n):
            a = mats[t]
            base = 8 * g
            a0 = a[g]
            qs, inside = pivots(a0, base, lane, sub)
            h, m, l = split3(a0)
            lhs = jnp.concatenate([h, h, m, h, l, m], axis=0).astype(jnp.bfloat16)
            h, m, l = split3(qs)
            rhs = jnp.concatenate([h, m, h, l, h, m], axis=0).astype(jnp.bfloat16)
            upd = lax.dot_general(lhs, rhs, (((0,), (0,)), ((), ())), preferred_element_type=jnp.float32)
            new = []
            for i in range(16):
                if i == g:
                    v = qs
                elif i == g + 1:
                    v = jnp.where(inside, 0.0, a[i])
                    t1 = v - lanes(a[i], base) * subl(qs, 0)
                    t2 = lanes(a[i], base + 1) * subl(qs, 1)
                    for m in range(2, 8, 2):
                        t1 = t1 - lanes(a[i], base + m) * subl(qs, m)
                        t2 = t2 + lanes(a[i], base + m + 1) * subl(qs, m + 1)
                    v = t1 - t2
                else:
                    v = jnp.where(inside, 0.0, a[i]) - upd[8 * i:8 * i + 8]
                new.append(v)
            mats[t] = new
        yield None
    yield [-jnp.concatenate(a, axis=0) for a in mats]


def dot(a, b, ca=1, cb=0):
    return lax.dot_general(a, b, (((ca,), (cb,)), ((), ())), precision=HI, preferred_element_type=jnp.float32)


MESH = pl.DeviceIdType.MESH
FOLDS = 5
BLOCK = 512
TRAITS = 8
CHUNKS = [[0, 1], [2, 3], [4, 5], [6, 7], [8], [9]]
XY_CHUNK = 1
FIRST = 4
Z_FIRST = (4, 5)
LEAD = 0
STEPS = len(CHUNKS)
ROWS = [16 * len(c) + (8 if i == XY_CHUNK else 0) for i, c in enumerate(CHUNKS)]
START = [sum(ROWS[:i]) for i in range(STEPS)]
TOTAL = sum(ROWS)
PLACE = {slot: START[i] + 16 * n for i, c in enumerate(CHUNKS) for n, slot in enumerate(c)}
XY_PLACE = START[XY_CHUNK] + 16 * len(CHUNKS[XY_CHUNK])


def fit_kernel(lam_ref, x_ref, yt_ref, fold_ref, beta_ref, out_ref, s_ref, t_ref, y_ref, b_ref, xv, lhs, part, relay, plain, comb, half, zin, quarters, done,
                load, send, recv, gsend, grecv):
    me = lax.axis_index("smp")
    fold_here = lax.rem(3 * me, 8)
    y, z = lax.div(me, 2), lax.rem(me, 2)
    right = lax.rem(y + 1, 4) * 2 + z
    left = lax.rem(y + 3, 4) * 2 + z
    across, after, before = lax.rem(y + 2, 4), lax.rem(y + 1, 4), lax.rem(y + 3, 4)
    other = y * 2 + (1 - z)
    barrier = pltpu.get_barrier_semaphore()
    loads = [pltpu.make_async_copy(x_ref.at[:, pl.ds(128 * p, 128)], xv.at[:, pl.ds(128 * p, 128)], load.at[p])
             for p in range(NB)]
    for c in loads:
        c.start()
    for i in range(1, 8):
        pl.semaphore_signal(barrier, inc=1, device_id={"smp": lax.rem(me + i, 8)}, device_id_type=MESH)

    @pl.when(fold_here >= FOLDS)
    def _():
        out_ref[...] = jnp.zeros_like(out_ref)

    y_rows = jnp.concatenate([yt_ref[...].astype(jnp.float32), jnp.zeros((8, x_ref.shape[0]), jnp.float32)], axis=0)
    y_rows = y_rows.astype(jnp.bfloat16)
    masks = [jnp.where(fold_ref[...] != k, 1.0, 0.0).astype(jnp.bfloat16) for k in range(FOLDS)]
    ready = set()

    def span(c):
        return pl.ds(FOLDS * START[c], FOLDS * ROWS[c])

    def hop(kind, c, src, dst, device):
        return pltpu.make_async_remote_copy(
            src_ref=src, dst_ref=dst, send_sem=send.at[kind, c], recv_sem=recv.at[kind, c],
            device_id={"smp": device}, device_id_type=MESH)

    def both(c):
        if c in Z_FIRST:
            n = FOLDS * ROWS[c] // 2
            return (4 * z, pl.ds(FOLDS * START[c], n)), (4 * z, pl.ds(FOLDS * START[c] + n, n))
        return (0, span(c)), (4, span(c))

    def relays(c):
        (zero, r0), (one, r1) = both(c)
        return [hop(0, c, part.at[zero + across, r0], relay.at[0, r0], right),
                hop(1, c, part.at[one + across, r1], relay.at[1, r1], left)]

    def plains(c):
        (zero, r0), (one, r1) = both(c)
        return [hop(2, c, part.at[one + after, r1], plain.at[0, r1], right),
                hop(3, c, part.at[zero + before, r0], plain.at[1, r0], left)]

    def combs(c):
        (zero, r0), (one, r1) = both(c)
        return [hop(4, c, relay.at[0, r0], comb.at[0, r0], right),
                hop(5, c, relay.at[1, r1], comb.at[1, r1], left)]

    def cross_z(c):
        if c in Z_FIRST:
            return hop(6, c, part.at[pl.ds(4 * (1 - z), 4), span(c)], quarters.at[:, span(c)], other)
        return hop(6, c, half.at[span(c)], zin.at[span(c)], other)

    def gather(c, k, sender):
        return pltpu.make_async_remote_copy(
            src_ref=done.at[pl.ds(FOLDS * START[c] + k * ROWS[c], ROWS[c])],
            dst_ref=out_ref.at[sender, pl.ds(START[c], ROWS[c])],
            send_sem=gsend.at[c, k], recv_sem=grecv.at[c, sender], device_id={"smp": 3 * k % 8}, device_id_type=MESH)

    def rows_of(p):
        if p in ready:
            return
        ready.add(p)
        loads[p].wait()
        xt = jnp.transpose(xv[:, 128 * p:128 * p + 128])
        for k in range(FOLDS):
            lhs[p, 128 * k:128 * k + 128, :] = xt * masks[k]

    def products(c):
        slots = CHUNKS[c]
        p, q = BLK[slots[0]]
        wide = len(slots) == 2 and BLK[slots[1]] == (p, q + 1)
        for n, slot in enumerate(slots):
            p, q = BLK[slot]
            rows_of(p)
            if q not in ready:
                rows_of(q)
            if wide and n == 0:
                rows_of(q + 1)
                both = jnp.dot(lhs[p], xv[:, 128 * q:128 * q + 256], preferred_element_type=jnp.float32)
            v = both[:, 128 * n:128 * n + 128] if wide else jnp.dot(
                lhs[p], xv[:, 128 * q:128 * q + 128], preferred_element_type=jnp.float32)
            for k in range(FOLDS):
                for s in range(8):
                    r = FOLDS * START[c] + k * ROWS[c] + 16 * n
                    part[s % 2 * 4 + s // 2, r:r + 16, :] = v[128 * k + 16 * s:128 * k + 16 * s + 16, :]
        if c == XY_CHUNK:
            for p in range(NB):
                rows_of(p)
            v = jnp.dot(jnp.concatenate([y_rows * m for m in masks], axis=0), xv[...], preferred_element_type=jnp.float32)
            for k in range(FOLDS):
                r = FOLDS * START[c] + (k + 1) * ROWS[c] - 8
                for s in range(8):
                    for q in range(NB):
                        part[s % 2 * 4 + s // 2, r + q:r + q + 1, :] = v[16 * k + s:16 * k + s + 1, 128 * q:128 * q + 128]
                    part[s % 2 * 4 + s // 2, r + 4:r + 8, :] = jnp.zeros((4, 128), jnp.float32)

    def arrived(g):
        @pl.when(fold_here < FOLDS)
        def _():
            def one(i, carry):
                gather(g, 0, lax.rem(me + i, 8)).wait_recv()
                return carry

            lax.fori_loop(1, 8, one, 0)

        row = lax.broadcasted_iota(jnp.int32, (128, 128), 0)
        col = lax.broadcasted_iota(jnp.int32, (128, 128), 1)
        for slot in CHUNKS[g]:
            p, q = BLK[slot]
            r = PLACE[slot]
            v = jnp.concatenate([out_ref[s, r:r + 16, :] for s in range(8)], axis=0)
            for j in range(2):
                w = v if p < q else v + jnp.where(row == col, lam_ref[j] * float(8 * x_ref.shape[0]), 0.0)
                s_ref[j, p, :, 128 * q:128 * q + 128] = w
        if g == XY_CHUNK:
            for s in range(8):
                for q in range(NB):
                    for j in range(2):
                        y_ref[j, s:s + 1, 128 * q:128 * q + 128] = out_ref[s, XY_PLACE + q:XY_PLACE + q + 1, :]

    def subtract(p, q, first, last):
        cols = slice(128 * first, 128 * last)
        for j in range(2):
            a = s_ref[j, p, :, 128 * q:128 * q + 128]
            s_ref[j, q, :, cols] = s_ref[j, q, :, cols] - dot(a, t_ref[j, p, :, cols], 0, 0)

    def eliminate(p, ws):
        lo, hi = 128 * p, 128 * p + 128
        for j in range(2):
            y = dot(y_ref[j, :, lo:hi], ws[j])
            y_ref[j, :, lo:hi] = y
            if p + 1 < NB:
                right = s_ref[j, p, :, hi:]
                t_ref[j, p, :, hi:] = dot(ws[j], right)
                y_ref[j, :, hi:] = y_ref[j, :, hi:] - dot(y, right)

    def diagonal(p):
        return inverse([s_ref[j, p, :, 128 * p:128 * p + 128] for j in range(2)])

    def tasks():
        arrived(0)
        for n, ws in enumerate(diagonal(0)):
            if n == 7:
                yield None
        arrived(1)
        eliminate(0, ws)
        yield None
        arrived(2)
        subtract(0, 1, 1, 3)
        for n, ws in enumerate(diagonal(1)):
            if n in (7, 15):
                yield None
        arrived(3)
        subtract(0, 1, 3, 4)
        eliminate(1, ws)
        subtract(0, 2, 2, 3)
        subtract(1, 2, 2, 3)
        for n, ws in enumerate(diagonal(2)):
            if n == 7:
                yield None
        arrived(4)
        subtract(0, 2, 3, 4)
        subtract(1, 2, 3, 4)
        eliminate(2, ws)
        arrived(5)
        for q in range(3):
            subtract(q, 3, 3, 4)
        for n, ws in enumerate(diagonal(3)):
            pass
        eliminate(3, ws)
        for p in range(NB - 2, -1, -1):
            lo, hi = 128 * p, 128 * p + 128
            for j in range(2):
                y_ref[j, :, lo:hi] = y_ref[j, :, lo:hi] - dot(y_ref[j, :, hi:], t_ref[j, p, :, hi:], 1, 1)
        for t in range(TRAITS):
            for j in range(2):
                b_ref[2 * t + j:2 * t + j + 1, :] = y_ref[j, t:t + 1, :]
        beta_ref[...] = b_ref[...].astype(jnp.bfloat16)

    solving = tasks()

    def send_relays(g):
        for c in relays(g) + plains(g):
            c.start()

    def send_combs(g):
        (zero, r0), (one, r1) = both(g)
        for c in relays(g):
            c.wait_recv()
        relay[0, r0] += part[zero + after, r0]
        relay[1, r1] += part[one + before, r1]
        for c in combs(g):
            c.start()

    def totals(g):
        (zero, r0), (one, r1) = both(g)
        for c in plains(g) + combs(g):
            c.wait_recv()
        return part[zero + y, r0] + plain[1, r0] + comb[0, r0], part[one + y, r1] + plain[0, r1] + comb[1, r1]

    def send_gathers(g):
        for k in range(FOLDS):
            @pl.when(fold_here != k)
            def _():
                gather(g, k, me).start()

            @pl.when(fold_here == k)
            def _():
                r = FOLDS * START[g] + k * ROWS[g]
                out_ref[me, START[g]:START[g] + ROWS[g], :] = done[r:r + ROWS[g], :]

    for i in range(STEPS + 3):
        if i < STEPS:
            if i in Z_FIRST:
                cross_z(i).wait_recv()
                for n in range(4):
                    part[4 * z + n, span(i)] += quarters[n, span(i)]
            else:
                products(i)
            if i == 0:
                pl.semaphore_wait(barrier, 7)
            send_relays(i)
            if 0 <= i - LEAD < len(Z_FIRST):
                products(Z_FIRST[i - LEAD])
                cross_z(Z_FIRST[i - LEAD]).start()
        if 1 <= i <= STEPS:
            send_combs(i - 1)
        if 2 <= i <= STEPS + 1:
            g = i - 2
            zero, one = totals(g)
            if g in Z_FIRST:
                n = FOLDS * ROWS[g] // 2
                done[FOLDS * START[g]:FOLDS * START[g] + n] = zero
                done[FOLDS * START[g] + n:FOLDS * START[g] + 2 * n] = one
                send_gathers(g)
            else:
                half[span(g)] = jnp.where(z == 0, one, zero)
                done[span(g)] = jnp.where(z == 0, zero, one)
                cross_z(g).start()
        if i >= 3 and i - 3 not in Z_FIRST:
            g = i - 3
            cross_z(g).wait_recv()
            done[span(g)] += zin[span(g)]
            send_gathers(g)
        if i >= FIRST:
            next(solving)

    for _ in solving:
        pass
    for g in range(STEPS):
        for c in relays(g) + plains(g) + combs(g) + [cross_z(g)]:
            c.wait_send()
        for k in range(FOLDS):
            @pl.when(fold_here != k)
            def _():
                gather(g, k, me).wait_send()


def fit(lam, x, yt, fold):
    vmem = pl.BlockSpec(memory_space=pltpu.VMEM)
    f32 = jnp.float32
    rows = FOLDS * TOTAL
    return pl.pallas_call(
        fit_kernel,
        out_shape=jax.ShapeDtypeStruct((16, BLOCK), jnp.bfloat16),
        in_specs=[pl.BlockSpec(memory_space=pltpu.SMEM), pl.BlockSpec(memory_space=pltpu.HBM), vmem, vmem],
        out_specs=vmem,
        scratch_shapes=[
            pltpu.VMEM((8, TOTAL, 128), f32),
            pltpu.VMEM((2, NB, 128, BLOCK), f32),
            pltpu.VMEM((2, NB, 128, BLOCK), f32),
            pltpu.VMEM((2, TRAITS, BLOCK), f32),
            pltpu.VMEM((16, BLOCK), f32),
            pltpu.VMEM(x.shape, jnp.bfloat16),
            pltpu.VMEM((NB, 128 * FOLDS, x.shape[0]), jnp.bfloat16),
            pltpu.VMEM((8, rows, 128), f32),
            pltpu.VMEM((2, rows, 128), f32),
            pltpu.VMEM((2, rows, 128), f32),
            pltpu.VMEM((2, rows, 128), f32),
            pltpu.VMEM((rows, 128), f32),
            pltpu.VMEM((rows, 128), f32),
            pltpu.VMEM((4, rows, 128), f32),
            pltpu.VMEM((rows, 128), f32),
            pltpu.SemaphoreType.DMA((NB,)),
            pltpu.SemaphoreType.DMA((7, STEPS)),
            pltpu.SemaphoreType.DMA((7, STEPS)),
            pltpu.SemaphoreType.DMA((STEPS, FOLDS)),
            pltpu.SemaphoreType.DMA((STEPS, 8)),
        ],
        compiler_params=pltpu.CompilerParams(collective_id=1, has_side_effects=True, vmem_limit_bytes=62 << 20),
    )(lam, x, yt, fold)


def tail_kernel(beta_ref, x_ref, fold_ref, old_ref, oof_ref, cross_ref, xv, betas, mine, feats, terms, rows, sums,
                load, bsend, brecv, fsend, frecv, tsend, trecv, ssend, srecv):
    s, b = lax.axis_index("smp"), lax.axis_index("blk")
    fold_here = lax.rem(3 * s, 8)
    samples = x_ref.shape[0]
    fetch = pltpu.make_async_copy(x_ref, xv, load.at[0])
    fetch.start()
    barrier = pltpu.get_barrier_semaphore()

    def greet_smp(i, carry):
        pl.semaphore_signal(barrier, inc=1, device_id={"smp": lax.rem(s + i, 8)}, device_id_type=MESH)
        return carry

    def greet_blk(i, carry):
        pl.semaphore_signal(barrier, inc=1, device_id={"blk": lax.rem(b + i, 16)}, device_id_type=MESH)
        return carry

    for i in range(1, 8):
        greet_smp(i, 0)
    for i in range(1, 16):
        greet_blk(i, 0)
    pl.semaphore_wait(barrier, 22)
    fetch.wait()

    def spread(i):
        return pltpu.make_async_remote_copy(
            src_ref=beta_ref, dst_ref=betas.at[fold_here], send_sem=bsend.at[i], recv_sem=brecv.at[fold_here],
            device_id={"smp": lax.rem(s + i, 8)}, device_id_type=MESH)

    def start_spread(i, carry):
        spread(i).start()
        return carry

    def end_spread(i, carry):
        spread(i).wait_send()
        return carry

    @pl.when(fold_here < FOLDS)
    def _():
        for i in range(1, 8):
            start_spread(i, 0)
        betas[fold_here] = beta_ref[...]

    def beta_in(k, carry):
        @pl.when(fold_here != k)
        def _():
            pltpu.make_async_remote_copy(
                src_ref=beta_ref, dst_ref=betas.at[k], send_sem=bsend.at[0], recv_sem=brecv.at[k],
                device_id={"smp": lax.rem(s + 1, 8)}, device_id_type=MESH).wait_recv()
        return carry

    for k in range(FOLDS):
        beta_in(k, 0)
    flat = jnp.concatenate([betas[k] for k in range(FOLDS)], axis=0)
    fitted = lax.dot_general(flat, xv[...], (((1,), (1,)), ((), ())), preferred_element_type=jnp.float32)
    fold = fold_ref[...]
    chosen = jnp.zeros((16, samples), jnp.float32)
    for k in range(FOLDS):
        chosen = jnp.where(fold == k, fitted[16 * k:16 * k + 16, :], chosen)
    oof = (chosen * math.sqrt(8 * samples / BLOCK)).astype(jnp.bfloat16)
    oof_ref[...] = oof
    for c in range(16):
        mine[c] = oof[:, 128 * c:128 * c + 128]
    feats[b] = mine[b]

    def feature(i):
        to = lax.rem(b + i, 16)
        return pltpu.make_async_remote_copy(
            src_ref=mine.at[to], dst_ref=feats.at[b], send_sem=fsend.at[i], recv_sem=frecv.at[i],
            device_id={"blk": to}, device_id_type=MESH)

    def start_feature(i, carry):
        feature(i).start()
        return carry

    def end_feature(i, carry):
        feature(i).wait()
        return carry

    for i in range(1, 16):
        start_feature(i, 0)
    r = lax.broadcasted_iota(jnp.int32, (256, 512), 0)
    c = lax.broadcasted_iota(jnp.int32, (256, 512), 1)
    same = ((r >> 1) & 7) == jnp.where(c < 256, c >> 5, (c >> 1) & 7)
    r = lax.broadcasted_iota(jnp.int32, (512, 128), 0)
    c = lax.broadcasted_iota(jnp.int32, (512, 128), 1)
    place = jnp.where(r < 256, r & 31, 32 + (((r - 256) >> 4) << 1) + (r & 1))
    pick = jnp.where(place == c, 1.0, 0.0).astype(jnp.bfloat16)
    for i in range(1, 16):
        end_feature(i, 0)
    f = jnp.concatenate([feats[c] for c in range(16)], axis=0)
    nt = (((1,), (1,)), ((), ()))
    against = lax.dot_general(f, jnp.concatenate([old_ref[...], f], axis=0), nt, preferred_element_type=jnp.float32)
    chosen = jnp.where(same, against, 0.0)
    hi = chosen.astype(jnp.bfloat16)
    rest = chosen - hi.astype(jnp.float32)
    mid = rest.astype(jnp.bfloat16)
    low = (rest - mid.astype(jnp.float32)).astype(jnp.bfloat16)
    total = jnp.dot(hi, pick, preferred_element_type=jnp.float32)
    total += jnp.dot(mid, pick, preferred_element_type=jnp.float32)
    total += jnp.dot(low, pick, preferred_element_type=jnp.float32)
    for k in range(16):
        terms[k] = total[16 * k:16 * k + 16, :]
    rows[b] = terms[b]

    def term(i):
        to = lax.rem(b + i, 16)
        return pltpu.make_async_remote_copy(
            src_ref=terms.at[to], dst_ref=rows.at[b], send_sem=tsend.at[i], recv_sem=trecv.at[i],
            device_id={"blk": to}, device_id_type=MESH)

    def start_term(i, carry):
        term(i).start()
        return carry

    def end_term(i, carry):
        term(i).wait()
        return carry

    for i in range(1, 16):
        start_term(i, 0)
    for i in range(1, 16):
        end_term(i, 0)
    part = rows[0]
    for k in range(1, 16):
        part = part + rows[k]
    sums[s] = part

    def last(i):
        return pltpu.make_async_remote_copy(
            src_ref=sums.at[s], dst_ref=sums.at[s], send_sem=ssend.at[i], recv_sem=srecv.at[i],
            device_id={"smp": lax.rem(s + i, 8)}, device_id_type=MESH)

    def start_last(i, carry):
        last(i).start()
        return carry

    def end_last(i, carry):
        last(i).wait()
        return carry

    for i in range(1, 8):
        start_last(i, 0)
    for i in range(1, 8):
        end_last(i, 0)
    final = sums[0]
    for k in range(1, 8):
        final = final + sums[k]
    cross_ref[...] = final * (1.0 / (8 * samples))

    @pl.when(fold_here < FOLDS)
    def _():
        for i in range(1, 8):
            end_spread(i, 0)


def tail(beta, x, fold, old):
    vmem = pl.BlockSpec(memory_space=pltpu.VMEM)
    dma = pltpu.SemaphoreType.DMA
    return pl.pallas_call(
        tail_kernel,
        out_shape=(jax.ShapeDtypeStruct((16, x.shape[0]), jnp.bfloat16), jax.ShapeDtypeStruct((16, 128), jnp.float32)),
        in_specs=[vmem, pl.BlockSpec(memory_space=pltpu.HBM), vmem, vmem],
        out_specs=(vmem, vmem),
        scratch_shapes=[
            pltpu.VMEM(x.shape, jnp.bfloat16),
            pltpu.VMEM((FOLDS, 16, BLOCK), jnp.bfloat16),
            pltpu.VMEM((16, 16, 128), jnp.bfloat16),
            pltpu.VMEM((16, 16, 128), jnp.bfloat16),
            pltpu.VMEM((16, 16, 128), jnp.float32),
            pltpu.VMEM((16, 16, 128), jnp.float32),
            pltpu.VMEM((8, 16, 128), jnp.float32),
            dma((1,)), dma((8,)), dma((8,)), dma((16,)), dma((16,)), dma((16,)), dma((16,)), dma((8,)), dma((8,)),
        ],
        compiler_params=pltpu.CompilerParams(collective_id=2, has_side_effects=True, vmem_limit_bytes=62 << 20),
    )(beta, x, fold, old)


def local(x, y, fold, lam, old):
    rows = x.shape[0]
    fold = fold[None, :]
    beta = fit(lam, x, y.T, fold)
    before = jnp.transpose(old[0], (1, 2, 0)).reshape(256, 128)
    oof, cross = tail(beta, x, fold, before)
    here = lax.dynamic_slice_in_dim(cross, 8 * lax.axis_index("smp"), 8, 1)
    return jnp.transpose(oof.reshape(TRAITS, 2, rows), (2, 0, 1)), here.reshape(TRAITS, 2, 8)


def solution(mesh):
    return jax.shard_map(
        local,
        mesh=mesh,
        in_specs=(P("smp", "blk"), P("smp", None), P("smp"), P(), P("smp", "blk", None, None)),
        out_specs=(P("smp", None, "blk"), P(None, "blk", "smp")),
        check_vma=False,
    )
```

```python
import math

import jax
import jax.numpy as jnp
from jax import lax
from jax.experimental import pallas as pl
from jax.experimental.pallas import tpu as pltpu
from jax.sharding import PartitionSpec as P

HI = lax.Precision.HIGHEST
NB = 4
BLK = [(p, q) for p in range(NB) for q in range(p, NB)]
IDX = {pq: i for i, pq in enumerate(BLK)}


def lanes(x, m):
    return jnp.broadcast_to(x[:, m:m + 1], x.shape)


def subl(x, m):
    return jnp.broadcast_to(x[m:m + 1, :], x.shape)


def split3(x):
    hi = x.astype(jnp.bfloat16).astype(jnp.float32)
    r = x - hi
    mid = r.astype(jnp.bfloat16).astype(jnp.float32)
    return hi, mid, r - mid


def pivots(a0, base, lane, sub):
    cols = [lanes(a0, base + m) for m in range(8)]
    inside = (lane >= base) & (lane < base + 8)
    z = jnp.where(inside, jnp.where(lane - base == sub, -1.0, 0.0), a0)
    scale = None
    for m in range(8):
        d = 1.0 / subl(cols[m], m)
        l = jnp.where(sub == m, 0.0, cols[m] * d)
        z = z - l * subl(z, m)
        for j in range(m + 1, 8):
            cols[j] = cols[j] - l * subl(cols[j], m)
        scale = d if m == 0 else jnp.where(sub == m, d, scale)
    return z * scale, inside


def inverse(mats):
    n = len(mats)
    lane = lax.broadcasted_iota(jnp.int32, (8, 128), 1)
    sub = lax.broadcasted_iota(jnp.int32, (8, 128), 0)
    mats = [[a[8 * i:8 * i + 8] for i in range(16)] for a in mats]
    for g in range(16):
        for t in range(n):
            a = mats[t]
            base = 8 * g
            a0 = a[g]
            qs, inside = pivots(a0, base, lane, sub)
            h, m, l = split3(a0)
            lhs = jnp.concatenate([h, h, m, h, l, m], axis=0).astype(jnp.bfloat16)
            h, m, l = split3(qs)
            rhs = jnp.concatenate([h, m, h, l, h, m], axis=0).astype(jnp.bfloat16)
            upd = lax.dot_general(lhs, rhs, (((0,), (0,)), ((), ())), preferred_element_type=jnp.float32)
            new = []
            for i in range(16):
                if i == g:
                    v = qs
                elif i == g + 1:
                    v = jnp.where(inside, 0.0, a[i])
                    t1 = v - lanes(a[i], base) * subl(qs, 0)
                    t2 = lanes(a[i], base + 1) * subl(qs, 1)
                    for m in range(2, 8, 2):
                        t1 = t1 - lanes(a[i], base + m) * subl(qs, m)
                        t2 = t2 + lanes(a[i], base + m + 1) * subl(qs, m + 1)
                    v = t1 - t2
                else:
                    v = jnp.where(inside, 0.0, a[i]) - upd[8 * i:8 * i + 8]
                new.append(v)
            mats[t] = new
        yield None
    yield [-jnp.concatenate(a, axis=0) for a in mats]


def dot(a, b, ca=1, cb=0):
    return lax.dot_general(a, b, (((ca,), (cb,)), ((), ())), precision=HI, preferred_element_type=jnp.float32)


MESH = pl.DeviceIdType.MESH
FOLDS = 5
BLOCK = 512
TRAITS = 8
CHUNKS = [[0, 1], [2, 3], [4, 5], [6, 7], [8], [9]]
XY_CHUNK = 1
FIRST = 4
Z_FIRST = (4, 5)
LEAD = 0
STEPS = len(CHUNKS)
ROWS = [16 * len(c) + (8 if i == XY_CHUNK else 0) for i, c in enumerate(CHUNKS)]
START = [sum(ROWS[:i]) for i in range(STEPS)]
TOTAL = sum(ROWS)
PLACE = {slot: START[i] + 16 * n for i, c in enumerate(CHUNKS) for n, slot in enumerate(c)}
XY_PLACE = START[XY_CHUNK] + 16 * len(CHUNKS[XY_CHUNK])


def fit_kernel(lam_ref, x_ref, yt_ref, fold_ref, beta_ref, out_ref, s_ref, t_ref, y_ref, b_ref, xv, lhs, part, relay, plain, comb, half, zin, quarters, done,
                load, send, recv, gsend, grecv):
    me = lax.axis_index("smp")
    fold_here = lax.rem(3 * me, 8)
    y, z = lax.div(me, 2), lax.rem(me, 2)
    right = lax.rem(y + 1, 4) * 2 + z
    left = lax.rem(y + 3, 4) * 2 + z
    across, after, before = lax.rem(y + 2, 4), lax.rem(y + 1, 4), lax.rem(y + 3, 4)
    other = y * 2 + (1 - z)
    barrier = pltpu.get_barrier_semaphore()
    loads = [pltpu.make_async_copy(x_ref.at[:, pl.ds(128 * p, 128)], xv.at[:, pl.ds(128 * p, 128)], load.at[p])
             for p in range(NB)]
    for c in loads:
        c.start()
    for i in range(1, 8):
        pl.semaphore_signal(barrier, inc=1, device_id={"smp": lax.rem(me + i, 8)}, device_id_type=MESH)

    @pl.when(fold_here >= FOLDS)
    def _():
        out_ref[...] = jnp.zeros_like(out_ref)

    y_rows = jnp.concatenate([yt_ref[...].astype(jnp.float32), jnp.zeros((8, x_ref.shape[0]), jnp.float32)], axis=0)
    y_rows = y_rows.astype(jnp.bfloat16)
    masks = [jnp.where(fold_ref[...] != k, 1.0, 0.0).astype(jnp.bfloat16) for k in range(FOLDS)]
    ready = set()

    def span(c):
        return pl.ds(FOLDS * START[c], FOLDS * ROWS[c])

    def hop(kind, c, src, dst, device):
        return pltpu.make_async_remote_copy(
            src_ref=src, dst_ref=dst, send_sem=send.at[kind, c], recv_sem=recv.at[kind, c],
            device_id={"smp": device}, device_id_type=MESH)

    def both(c):
        if c in Z_FIRST:
            n = FOLDS * ROWS[c] // 2
            return (4 * z, pl.ds(FOLDS * START[c], n)), (4 * z, pl.ds(FOLDS * START[c] + n, n))
        return (0, span(c)), (4, span(c))

    def relays(c):
        (zero, r0), (one, r1) = both(c)
        return [hop(0, c, part.at[zero + across, r0], relay.at[0, r0], right),
                hop(1, c, part.at[one + across, r1], relay.at[1, r1], left)]

    def plains(c):
        (zero, r0), (one, r1) = both(c)
        return [hop(2, c, part.at[one + after, r1], plain.at[0, r1], right),
                hop(3, c, part.at[zero + before, r0], plain.at[1, r0], left)]

    def combs(c):
        (zero, r0), (one, r1) = both(c)
        return [hop(4, c, relay.at[0, r0], comb.at[0, r0], right),
                hop(5, c, relay.at[1, r1], comb.at[1, r1], left)]

    def cross_z(c):
        if c in Z_FIRST:
            return hop(6, c, part.at[pl.ds(4 * (1 - z), 4), span(c)], quarters.at[:, span(c)], other)
        return hop(6, c, half.at[span(c)], zin.at[span(c)], other)

    def gather(c, k, sender):
        return pltpu.make_async_remote_copy(
            src_ref=done.at[pl.ds(FOLDS * START[c] + k * ROWS[c], ROWS[c])],
            dst_ref=out_ref.at[sender, pl.ds(START[c], ROWS[c])],
            send_sem=gsend.at[c, k], recv_sem=grecv.at[c, sender], device_id={"smp": 3 * k % 8}, device_id_type=MESH)

    def rows_of(p):
        if p in ready:
            return
        ready.add(p)
        loads[p].wait()
        xt = jnp.transpose(xv[:, 128 * p:128 * p + 128])
        for k in range(FOLDS):
            lhs[p, 128 * k:128 * k + 128, :] = xt * masks[k]

    def products(c):
        slots = CHUNKS[c]
        p, q = BLK[slots[0]]
        wide = len(slots) == 2 and BLK[slots[1]] == (p, q + 1)
        for n, slot in enumerate(slots):
            p, q = BLK[slot]
            rows_of(p)
            if q not in ready:
                rows_of(q)
            if wide and n == 0:
                rows_of(q + 1)
                both = jnp.dot(lhs[p], xv[:, 128 * q:128 * q + 256], preferred_element_type=jnp.float32)
            v = both[:, 128 * n:128 * n + 128] if wide else jnp.dot(
                lhs[p], xv[:, 128 * q:128 * q + 128], preferred_element_type=jnp.float32)
            for k in range(FOLDS):
                for s in range(8):
                    r = FOLDS * START[c] + k * ROWS[c] + 16 * n
                    part[s % 2 * 4 + s // 2, r:r + 16, :] = v[128 * k + 16 * s:128 * k + 16 * s + 16, :]
        if c == XY_CHUNK:
            for p in range(NB):
                rows_of(p)
            v = jnp.dot(jnp.concatenate([y_rows * m for m in masks], axis=0), xv[...], preferred_element_type=jnp.float32)
            for k in range(FOLDS):
                r = FOLDS * START[c] + (k + 1) * ROWS[c] - 8
                for s in range(8):
                    for q in range(NB):
                        part[s % 2 * 4 + s // 2, r + q:r + q + 1, :] = v[16 * k + s:16 * k + s + 1, 128 * q:128 * q + 128]
                    part[s % 2 * 4 + s // 2, r + 4:r + 8, :] = jnp.zeros((4, 128), jnp.float32)

    def arrived(g):
        @pl.when(fold_here < FOLDS)
        def _():
            def one(i, carry):
                gather(g, 0, lax.rem(me + i, 8)).wait_recv()
                return carry

            lax.fori_loop(1, 8, one, 0)

        row = lax.broadcasted_iota(jnp.int32, (128, 128), 0)
        col = lax.broadcasted_iota(jnp.int32, (128, 128), 1)
        for slot in CHUNKS[g]:
            p, q = BLK[slot]
            r = PLACE[slot]
            v = jnp.concatenate([out_ref[s, r:r + 16, :] for s in range(8)], axis=0)
            for j in range(2):
                w = v if p < q else v + jnp.where(row == col, lam_ref[j] * float(8 * x_ref.shape[0]), 0.0)
                s_ref[j, p, :, 128 * q:128 * q + 128] = w
        if g == XY_CHUNK:
            for s in range(8):
                for q in range(NB):
                    for j in range(2):
                        y_ref[j, s:s + 1, 128 * q:128 * q + 128] = out_ref[s, XY_PLACE + q:XY_PLACE + q + 1, :]

    def subtract(p, q, first, last):
        cols = slice(128 * first, 128 * last)
        for j in range(2):
            a = s_ref[j, p, :, 128 * q:128 * q + 128]
            s_ref[j, q, :, cols] = s_ref[j, q, :, cols] - dot(a, t_ref[j, p, :, cols], 0, 0)

    def eliminate(p, ws):
        lo, hi = 128 * p, 128 * p + 128
        for j in range(2):
            y = dot(y_ref[j, :, lo:hi], ws[j])
            y_ref[j, :, lo:hi] = y
            if p + 1 < NB:
                right = s_ref[j, p, :, hi:]
                t_ref[j, p, :, hi:] = dot(ws[j], right)
                y_ref[j, :, hi:] = y_ref[j, :, hi:] - dot(y, right)

    def diagonal(p):
        return inverse([s_ref[j, p, :, 128 * p:128 * p + 128] for j in range(2)])

    def tasks():
        arrived(0)
        for n, ws in enumerate(diagonal(0)):
            if n == 7:
                yield None
        arrived(1)
        eliminate(0, ws)
        yield None
        arrived(2)
        subtract(0, 1, 1, 3)
        for n, ws in enumerate(diagonal(1)):
            if n in (7, 15):
                yield None
        arrived(3)
        subtract(0, 1, 3, 4)
        eliminate(1, ws)
        subtract(0, 2, 2, 3)
        subtract(1, 2, 2, 3)
        for n, ws in enumerate(diagonal(2)):
            if n == 7:
                yield None
                arrived(4)
                arrived(5)
                for q in (2, 3):
                    subtract(0, q, 3, 4)
                    subtract(1, q, 3, 4)
        eliminate(2, ws)
        subtract(2, 3, 3, 4)
        for n, ws in enumerate(diagonal(3)):
            pass
        eliminate(3, ws)
        for p in range(NB - 2, -1, -1):
            lo, hi = 128 * p, 128 * p + 128
            for j in range(2):
                y_ref[j, :, lo:hi] = y_ref[j, :, lo:hi] - dot(y_ref[j, :, hi:], t_ref[j, p, :, hi:], 1, 1)
        for t in range(TRAITS):
            for j in range(2):
                b_ref[2 * t + j:2 * t + j + 1, :] = y_ref[j, t:t + 1, :]
        beta_ref[...] = b_ref[...].astype(jnp.bfloat16)

    solving = tasks()

    def send_relays(g):
        for c in relays(g) + plains(g):
            c.start()

    def send_combs(g):
        (zero, r0), (one, r1) = both(g)
        for c in relays(g):
            c.wait_recv()
        relay[0, r0] += part[zero + after, r0]
        relay[1, r1] += part[one + before, r1]
        for c in combs(g):
            c.start()

    def totals(g):
        (zero, r0), (one, r1) = both(g)
        for c in plains(g) + combs(g):
            c.wait_recv()
        return part[zero + y, r0] + plain[1, r0] + comb[0, r0], part[one + y, r1] + plain[0, r1] + comb[1, r1]

    def send_gathers(g):
        for k in range(FOLDS):
            @pl.when(fold_here != k)
            def _():
                gather(g, k, me).start()

            @pl.when(fold_here == k)
            def _():
                r = FOLDS * START[g] + k * ROWS[g]
                out_ref[me, START[g]:START[g] + ROWS[g], :] = done[r:r + ROWS[g], :]

    for i in range(STEPS + 3):
        if i < STEPS:
            if i in Z_FIRST:
                cross_z(i).wait_recv()
                for n in range(4):
                    part[4 * z + n, span(i)] += quarters[n, span(i)]
            else:
                products(i)
            if i == 0:
                pl.semaphore_wait(barrier, 7)
            send_relays(i)
            if 0 <= i - LEAD < len(Z_FIRST):
                products(Z_FIRST[i - LEAD])
                cross_z(Z_FIRST[i - LEAD]).start()
        if 1 <= i <= STEPS:
            send_combs(i - 1)
        if 2 <= i <= STEPS + 1:
            g = i - 2
            zero, one = totals(g)
            if g in Z_FIRST:
                n = FOLDS * ROWS[g] // 2
                done[FOLDS * START[g]:FOLDS * START[g] + n] = zero
                done[FOLDS * START[g] + n:FOLDS * START[g] + 2 * n] = one
                send_gathers(g)
            else:
                half[span(g)] = jnp.where(z == 0, one, zero)
                done[span(g)] = jnp.where(z == 0, zero, one)
                cross_z(g).start()
        if i >= 3 and i - 3 not in Z_FIRST:
            g = i - 3
            cross_z(g).wait_recv()
            done[span(g)] += zin[span(g)]
            send_gathers(g)
        if i >= FIRST:
            next(solving)

    for _ in solving:
        pass
    for g in range(STEPS):
        for c in relays(g) + plains(g) + combs(g) + [cross_z(g)]:
            c.wait_send()
        for k in range(FOLDS):
            @pl.when(fold_here != k)
            def _():
                gather(g, k, me).wait_send()


def fit(lam, x, yt, fold):
    vmem = pl.BlockSpec(memory_space=pltpu.VMEM)
    f32 = jnp.float32
    rows = FOLDS * TOTAL
    return pl.pallas_call(
        fit_kernel,
        out_shape=jax.ShapeDtypeStruct((16, BLOCK), jnp.bfloat16),
        in_specs=[pl.BlockSpec(memory_space=pltpu.SMEM), pl.BlockSpec(memory_space=pltpu.HBM), vmem, vmem],
        out_specs=vmem,
        scratch_shapes=[
            pltpu.VMEM((8, TOTAL, 128), f32),
            pltpu.VMEM((2, NB, 128, BLOCK), f32),
            pltpu.VMEM((2, NB, 128, BLOCK), f32),
            pltpu.VMEM((2, TRAITS, BLOCK), f32),
            pltpu.VMEM((16, BLOCK), f32),
            pltpu.VMEM(x.shape, jnp.bfloat16),
            pltpu.VMEM((NB, 128 * FOLDS, x.shape[0]), jnp.bfloat16),
            pltpu.VMEM((8, rows, 128), f32),
            pltpu.VMEM((2, rows, 128), f32),
            pltpu.VMEM((2, rows, 128), f32),
            pltpu.VMEM((2, rows, 128), f32),
            pltpu.VMEM((rows, 128), f32),
            pltpu.VMEM((rows, 128), f32),
            pltpu.VMEM((4, rows, 128), f32),
            pltpu.VMEM((rows, 128), f32),
            pltpu.SemaphoreType.DMA((NB,)),
            pltpu.SemaphoreType.DMA((7, STEPS)),
            pltpu.SemaphoreType.DMA((7, STEPS)),
            pltpu.SemaphoreType.DMA((STEPS, FOLDS)),
            pltpu.SemaphoreType.DMA((STEPS, 8)),
        ],
        compiler_params=pltpu.CompilerParams(collective_id=1, has_side_effects=True, vmem_limit_bytes=62 << 20),
    )(lam, x, yt, fold)


def tail_kernel(beta_ref, x_ref, fold_ref, old_ref, oof_ref, cross_ref, xv, fv, ov, betas, mine, feats, terms, rows, sums,
                load, bsend, brecv, fsend, frecv, tsend, trecv, ssend, srecv):
    s, b = lax.axis_index("smp"), lax.axis_index("blk")
    fold_here = lax.rem(3 * s, 8)
    samples = x_ref.shape[0]
    fetches = [pltpu.make_async_copy(x_ref, xv, load.at[0]), pltpu.make_async_copy(fold_ref, fv, load.at[1]),
               pltpu.make_async_copy(old_ref, ov, load.at[2])]
    for fetch in fetches:
        fetch.start()
    barrier = pltpu.get_barrier_semaphore()

    def greet_smp(i, carry):
        pl.semaphore_signal(barrier, inc=1, device_id={"smp": lax.rem(s + i, 8)}, device_id_type=MESH)
        return carry

    def greet_blk(i, carry):
        pl.semaphore_signal(barrier, inc=1, device_id={"blk": lax.rem(b + i, 16)}, device_id_type=MESH)
        return carry

    for i in range(1, 8):
        greet_smp(i, 0)
    for i in range(1, 16):
        greet_blk(i, 0)
    pl.semaphore_wait(barrier, 22)

    def spread(i):
        return pltpu.make_async_remote_copy(
            src_ref=beta_ref, dst_ref=betas.at[fold_here], send_sem=bsend.at[i], recv_sem=brecv.at[fold_here],
            device_id={"smp": lax.rem(s + i, 8)}, device_id_type=MESH)

    def start_spread(i, carry):
        spread(i).start()
        return carry

    def end_spread(i, carry):
        spread(i).wait_send()
        return carry

    @pl.when(fold_here < FOLDS)
    def _():
        for i in range(1, 8):
            start_spread(i, 0)
        betas[fold_here] = beta_ref[...]

    def beta_in(k, carry):
        @pl.when(fold_here != k)
        def _():
            pltpu.make_async_remote_copy(
                src_ref=beta_ref, dst_ref=betas.at[k], send_sem=bsend.at[0], recv_sem=brecv.at[k],
                device_id={"smp": lax.rem(s + 1, 8)}, device_id_type=MESH).wait_recv()
        return carry

    for fetch in fetches:
        fetch.wait()
    for k in range(FOLDS):
        beta_in(k, 0)
    flat = jnp.concatenate([betas[k] for k in range(FOLDS)], axis=0)
    fitted = lax.dot_general(flat, xv[...], (((1,), (1,)), ((), ())), preferred_element_type=jnp.float32)
    fold = fv[...]
    chosen = jnp.zeros((16, samples), jnp.float32)
    for k in range(FOLDS):
        chosen = jnp.where(fold == k, fitted[16 * k:16 * k + 16, :], chosen)
    oof = (chosen * math.sqrt(8 * samples / BLOCK)).astype(jnp.bfloat16)
    for c in range(16):
        mine[c] = oof[:, 128 * c:128 * c + 128]
    feats[b] = mine[b]

    def feature(i):
        to = lax.rem(b + i, 16)
        return pltpu.make_async_remote_copy(
            src_ref=mine.at[to], dst_ref=feats.at[b], send_sem=fsend.at[i], recv_sem=frecv.at[i],
            device_id={"blk": to}, device_id_type=MESH)

    def start_feature(i, carry):
        feature(i).start()
        return carry

    def end_feature(i, carry):
        feature(i).wait_recv()
        return carry

    for i in range(1, 16):
        start_feature(i, 0)
    oof_ref[...] = oof
    r = lax.broadcasted_iota(jnp.int32, (256, 512), 0)
    c = lax.broadcasted_iota(jnp.int32, (256, 512), 1)
    same = ((r >> 1) & 7) == jnp.where(c < 256, c >> 5, (c >> 1) & 7)
    r = lax.broadcasted_iota(jnp.int32, (512, 128), 0)
    c = lax.broadcasted_iota(jnp.int32, (512, 128), 1)
    place = jnp.where(r < 256, r & 31, 32 + (((r - 256) >> 4) << 1) + (r & 1))
    pick = jnp.where(place == c, 1.0, 0.0).astype(jnp.bfloat16)
    for i in range(1, 16):
        end_feature(i, 0)
    f = jnp.concatenate([feats[c] for c in range(16)], axis=0)
    nt = (((1,), (1,)), ((), ()))
    against = lax.dot_general(f, jnp.concatenate([ov[...], f], axis=0), nt, preferred_element_type=jnp.float32)
    chosen = jnp.where(same, against, 0.0)
    hi = chosen.astype(jnp.bfloat16)
    rest = chosen - hi.astype(jnp.float32)
    mid = rest.astype(jnp.bfloat16)
    low = (rest - mid.astype(jnp.float32)).astype(jnp.bfloat16)
    total = jnp.dot(hi, pick, preferred_element_type=jnp.float32)
    total += jnp.dot(mid, pick, preferred_element_type=jnp.float32)
    total += jnp.dot(low, pick, preferred_element_type=jnp.float32)
    for k in range(16):
        terms[k] = total[16 * k:16 * k + 16, :]
    rows[b] = terms[b]

    def term(i):
        to = lax.rem(b + i, 16)
        return pltpu.make_async_remote_copy(
            src_ref=terms.at[to], dst_ref=rows.at[b], send_sem=tsend.at[i], recv_sem=trecv.at[i],
            device_id={"blk": to}, device_id_type=MESH)

    def start_term(i, carry):
        term(i).start()
        return carry

    def end_term(i, carry):
        term(i).wait_recv()
        return carry

    for i in range(1, 16):
        start_term(i, 0)
    for i in range(1, 16):
        end_term(i, 0)
    part = rows[0]
    for k in range(1, 16):
        part = part + rows[k]
    sums[s] = part

    def last(i):
        return pltpu.make_async_remote_copy(
            src_ref=sums.at[s], dst_ref=sums.at[s], send_sem=ssend.at[i], recv_sem=srecv.at[i],
            device_id={"smp": lax.rem(s + i, 8)}, device_id_type=MESH)

    def start_last(i, carry):
        last(i).start()
        return carry

    def end_last(i, carry):
        last(i).wait_recv()
        return carry

    for i in range(1, 8):
        start_last(i, 0)
    for i in range(1, 8):
        end_last(i, 0)
    final = sums[0]
    for k in range(1, 8):
        final = final + sums[k]
    cross_ref[...] = final * (1.0 / (8 * samples))
    for i in range(1, 16):
        feature(i).wait_send()
        term(i).wait_send()
    for i in range(1, 8):
        last(i).wait_send()

    @pl.when(fold_here < FOLDS)
    def _():
        for i in range(1, 8):
            end_spread(i, 0)


def tail(beta, x, fold, old):
    vmem = pl.BlockSpec(memory_space=pltpu.VMEM)
    dma = pltpu.SemaphoreType.DMA
    return pl.pallas_call(
        tail_kernel,
        out_shape=(jax.ShapeDtypeStruct((16, x.shape[0]), jnp.bfloat16), jax.ShapeDtypeStruct((16, 128), jnp.float32)),
        in_specs=[vmem] + [pl.BlockSpec(memory_space=pltpu.HBM)] * 3,
        out_specs=(vmem, vmem),
        scratch_shapes=[
            pltpu.VMEM(x.shape, jnp.bfloat16),
            pltpu.VMEM(fold.shape, jnp.int32),
            pltpu.VMEM(old.shape, jnp.bfloat16),
            pltpu.VMEM((FOLDS, 16, BLOCK), jnp.bfloat16),
            pltpu.VMEM((16, 16, 128), jnp.bfloat16),
            pltpu.VMEM((16, 16, 128), jnp.bfloat16),
            pltpu.VMEM((16, 16, 128), jnp.float32),
            pltpu.VMEM((16, 16, 128), jnp.float32),
            pltpu.VMEM((8, 16, 128), jnp.float32),
            dma((3,)), dma((8,)), dma((8,)), dma((16,)), dma((16,)), dma((16,)), dma((16,)), dma((8,)), dma((8,)),
        ],
        compiler_params=pltpu.CompilerParams(collective_id=2, has_side_effects=True, vmem_limit_bytes=62 << 20),
    )(beta, x, fold, old)


def local(x, y, fold, lam, old):
    rows = x.shape[0]
    fold = fold[None, :]
    beta = fit(lam, x, y.T, fold)
    before = jnp.transpose(old[0], (1, 2, 0)).reshape(256, 128)
    oof, cross = tail(beta, x, fold, before)
    here = lax.dynamic_slice_in_dim(cross, 8 * lax.axis_index("smp"), 8, 1)
    return jnp.transpose(oof.reshape(TRAITS, 2, rows), (2, 0, 1)), here.reshape(TRAITS, 2, 8)


def solution(mesh):
    return jax.shard_map(
        local,
        mesh=mesh,
        in_specs=(P("smp", "blk"), P("smp", None), P("smp"), P(), P("smp", "blk", None, None)),
        out_specs=(P("smp", None, "blk"), P(None, "blk", "smp")),
        check_vma=False,
    )
```

```python
import math

import jax
import jax.numpy as jnp
from jax import lax
from jax.experimental import pallas as pl
from jax.experimental.pallas import tpu as pltpu
from jax.sharding import PartitionSpec as P

HI = lax.Precision.HIGHEST
NB = 4
BLK = [(p, q) for p in range(NB) for q in range(p, NB)]
IDX = {pq: i for i, pq in enumerate(BLK)}


def lanes(x, m):
    return jnp.broadcast_to(x[:, m:m + 1], x.shape)


def subl(x, m):
    return jnp.broadcast_to(x[m:m + 1, :], x.shape)


def split3(x):
    hi = x.astype(jnp.bfloat16).astype(jnp.float32)
    r = x - hi
    mid = r.astype(jnp.bfloat16).astype(jnp.float32)
    return hi, mid, r - mid


def pivots(a0, base, lane, sub):
    cols = [lanes(a0, base + m) for m in range(8)]
    inside = (lane >= base) & (lane < base + 8)
    z = jnp.where(inside, jnp.where(lane - base == sub, -1.0, 0.0), a0)
    scale = None
    for m in range(8):
        d = 1.0 / subl(cols[m], m)
        l = jnp.where(sub == m, 0.0, cols[m] * d)
        z = z - l * subl(z, m)
        for j in range(m + 1, 8):
            cols[j] = cols[j] - l * subl(cols[j], m)
        scale = d if m == 0 else jnp.where(sub == m, d, scale)
    return z * scale, inside


def inverse(mats):
    n = len(mats)
    lane = lax.broadcasted_iota(jnp.int32, (8, 128), 1)
    sub = lax.broadcasted_iota(jnp.int32, (8, 128), 0)
    mats = [[a[8 * i:8 * i + 8] for i in range(16)] for a in mats]
    for g in range(16):
        for t in range(n):
            a = mats[t]
            base = 8 * g
            a0 = a[g]
            qs, inside = pivots(a0, base, lane, sub)
            h, m, l = split3(a0)
            lhs = jnp.concatenate([h, h, m, h, l, m], axis=0).astype(jnp.bfloat16)
            h, m, l = split3(qs)
            rhs = jnp.concatenate([h, m, h, l, h, m], axis=0).astype(jnp.bfloat16)
            upd = lax.dot_general(lhs, rhs, (((0,), (0,)), ((), ())), preferred_element_type=jnp.float32)
            new = []
            for i in range(16):
                if i == g:
                    v = qs
                elif i == g + 1:
                    v = jnp.where(inside, 0.0, a[i])
                    t1 = v - lanes(a[i], base) * subl(qs, 0)
                    t2 = lanes(a[i], base + 1) * subl(qs, 1)
                    for m in range(2, 8, 2):
                        t1 = t1 - lanes(a[i], base + m) * subl(qs, m)
                        t2 = t2 + lanes(a[i], base + m + 1) * subl(qs, m + 1)
                    v = t1 - t2
                else:
                    v = jnp.where(inside, 0.0, a[i]) - upd[8 * i:8 * i + 8]
                new.append(v)
            mats[t] = new
        yield None
    yield [-jnp.concatenate(a, axis=0) for a in mats]


def dot(a, b, ca=1, cb=0):
    return lax.dot_general(a, b, (((ca,), (cb,)), ((), ())), precision=HI, preferred_element_type=jnp.float32)


MESH = pl.DeviceIdType.MESH
FOLDS = 5
BLOCK = 512
TRAITS = 8
CHUNKS = [[0, 1], [2, 3], [4, 5], [6, 7], [8], [9]]
XY_CHUNK = 1
FIRST = 4
Z_FIRST = (4, 5)
LEAD = 0
STEPS = len(CHUNKS)
ROWS = [16 * len(c) + (8 if i == XY_CHUNK else 0) for i, c in enumerate(CHUNKS)]
START = [sum(ROWS[:i]) for i in range(STEPS)]
TOTAL = sum(ROWS)
PLACE = {slot: START[i] + 16 * n for i, c in enumerate(CHUNKS) for n, slot in enumerate(c)}
XY_PLACE = START[XY_CHUNK] + 16 * len(CHUNKS[XY_CHUNK])


def fit_kernel(lam_ref, x_ref, yt_ref, fold_ref, beta_ref, out_ref, s_ref, t_ref, y_ref, b_ref, xv, lhs, part, relay, plain, comb, half, zin, quarters, done,
                load, send, recv, gsend, grecv):
    me = lax.axis_index("smp")
    fold_here = lax.rem(3 * me, 8)
    y, z = lax.div(me, 2), lax.rem(me, 2)
    right = lax.rem(y + 1, 4) * 2 + z
    left = lax.rem(y + 3, 4) * 2 + z
    across, after, before = lax.rem(y + 2, 4), lax.rem(y + 1, 4), lax.rem(y + 3, 4)
    other = y * 2 + (1 - z)
    barrier = pltpu.get_barrier_semaphore()
    loads = [pltpu.make_async_copy(x_ref.at[:, pl.ds(128 * p, 128)], xv.at[:, pl.ds(128 * p, 128)], load.at[p])
             for p in range(NB)]
    for c in loads:
        c.start()
    for i in range(1, 8):
        pl.semaphore_signal(barrier, inc=1, device_id={"smp": lax.rem(me + i, 8)}, device_id_type=MESH)

    @pl.when(fold_here >= FOLDS)
    def _():
        out_ref[...] = jnp.zeros_like(out_ref)

    y_rows = jnp.concatenate([yt_ref[...].astype(jnp.float32), jnp.zeros((8, x_ref.shape[0]), jnp.float32)], axis=0)
    y_rows = y_rows.astype(jnp.bfloat16)
    masks = [jnp.where(fold_ref[...] != k, 1.0, 0.0).astype(jnp.bfloat16) for k in range(FOLDS)]
    ready = set()

    def span(c):
        return pl.ds(FOLDS * START[c], FOLDS * ROWS[c])

    def hop(kind, c, src, dst, device):
        return pltpu.make_async_remote_copy(
            src_ref=src, dst_ref=dst, send_sem=send.at[kind, c], recv_sem=recv.at[kind, c],
            device_id={"smp": device}, device_id_type=MESH)

    def both(c):
        if c in Z_FIRST:
            n = FOLDS * ROWS[c] // 2
            return (4 * z, pl.ds(FOLDS * START[c], n)), (4 * z, pl.ds(FOLDS * START[c] + n, n))
        return (0, span(c)), (4, span(c))

    def relays(c):
        (zero, r0), (one, r1) = both(c)
        return [hop(0, c, part.at[zero + across, r0], relay.at[0, r0], right),
                hop(1, c, part.at[one + across, r1], relay.at[1, r1], left)]

    def plains(c):
        (zero, r0), (one, r1) = both(c)
        return [hop(2, c, part.at[one + after, r1], plain.at[0, r1], right),
                hop(3, c, part.at[zero + before, r0], plain.at[1, r0], left)]

    def combs(c):
        (zero, r0), (one, r1) = both(c)
        return [hop(4, c, relay.at[0, r0], comb.at[0, r0], right),
                hop(5, c, relay.at[1, r1], comb.at[1, r1], left)]

    def cross_z(c):
        if c in Z_FIRST:
            return hop(6, c, part.at[pl.ds(4 * (1 - z), 4), span(c)], quarters.at[:, span(c)], other)
        return hop(6, c, half.at[span(c)], zin.at[span(c)], other)

    def gather(c, k, sender):
        return pltpu.make_async_remote_copy(
            src_ref=done.at[pl.ds(FOLDS * START[c] + k * ROWS[c], ROWS[c])],
            dst_ref=out_ref.at[sender, pl.ds(START[c], ROWS[c])],
            send_sem=gsend.at[c, k], recv_sem=grecv.at[c, sender], device_id={"smp": 3 * k % 8}, device_id_type=MESH)

    def rows_of(p):
        if p in ready:
            return
        ready.add(p)
        loads[p].wait()
        xt = jnp.transpose(xv[:, 128 * p:128 * p + 128])
        for k in range(FOLDS):
            lhs[p, 128 * k:128 * k + 128, :] = xt * masks[k]

    def products(c):
        slots = CHUNKS[c]
        p, q = BLK[slots[0]]
        wide = len(slots) == 2 and BLK[slots[1]] == (p, q + 1)
        for n, slot in enumerate(slots):
            p, q = BLK[slot]
            rows_of(p)
            if q not in ready:
                rows_of(q)
            if wide and n == 0:
                rows_of(q + 1)
                both = jnp.dot(lhs[p], xv[:, 128 * q:128 * q + 256], preferred_element_type=jnp.float32)
            v = both[:, 128 * n:128 * n + 128] if wide else jnp.dot(
                lhs[p], xv[:, 128 * q:128 * q + 128], preferred_element_type=jnp.float32)
            for k in range(FOLDS):
                for s in range(8):
                    r = FOLDS * START[c] + k * ROWS[c] + 16 * n
                    part[s % 2 * 4 + s // 2, r:r + 16, :] = v[128 * k + 16 * s:128 * k + 16 * s + 16, :]
        if c == XY_CHUNK:
            for p in range(NB):
                rows_of(p)
            v = jnp.dot(jnp.concatenate([y_rows * m for m in masks], axis=0), xv[...], preferred_element_type=jnp.float32)
            for k in range(FOLDS):
                r = FOLDS * START[c] + (k + 1) * ROWS[c] - 8
                for s in range(8):
                    for q in range(NB):
                        part[s % 2 * 4 + s // 2, r + q:r + q + 1, :] = v[16 * k + s:16 * k + s + 1, 128 * q:128 * q + 128]
                    part[s % 2 * 4 + s // 2, r + 4:r + 8, :] = jnp.zeros((4, 128), jnp.float32)

    def arrived(g):
        @pl.when(fold_here < FOLDS)
        def _():
            def one(i, carry):
                gather(g, 0, lax.rem(me + i, 8)).wait_recv()
                return carry

            lax.fori_loop(1, 8, one, 0)

        row = lax.broadcasted_iota(jnp.int32, (128, 128), 0)
        col = lax.broadcasted_iota(jnp.int32, (128, 128), 1)
        for slot in CHUNKS[g]:
            p, q = BLK[slot]
            r = PLACE[slot]
            v = jnp.concatenate([out_ref[s, r:r + 16, :] for s in range(8)], axis=0)
            for j in range(2):
                w = v if p < q else v + jnp.where(row == col, lam_ref[j] * float(8 * x_ref.shape[0]), 0.0)
                s_ref[j, p, :, 128 * q:128 * q + 128] = w
        if g == XY_CHUNK:
            for s in range(8):
                for q in range(NB):
                    for j in range(2):
                        y_ref[j, s:s + 1, 128 * q:128 * q + 128] = out_ref[s, XY_PLACE + q:XY_PLACE + q + 1, :]

    def subtract(p, q, first, last):
        cols = slice(128 * first, 128 * last)
        for j in range(2):
            a = s_ref[j, p, :, 128 * q:128 * q + 128]
            s_ref[j, q, :, cols] = s_ref[j, q, :, cols] - dot(a, t_ref[j, p, :, cols], 0, 0)

    def eliminate(p, ws):
        lo, hi = 128 * p, 128 * p + 128
        for j in range(2):
            y = dot(y_ref[j, :, lo:hi], ws[j])
            y_ref[j, :, lo:hi] = y
            if p + 1 < NB:
                right = s_ref[j, p, :, hi:]
                t_ref[j, p, :, hi:] = dot(ws[j], right)
                y_ref[j, :, hi:] = y_ref[j, :, hi:] - dot(y, right)

    def diagonal(p):
        return inverse([s_ref[j, p, :, 128 * p:128 * p + 128] for j in range(2)])

    def tasks():
        arrived(0)
        for n, ws in enumerate(diagonal(0)):
            if n == 7:
                yield None
        arrived(1)
        eliminate(0, ws)
        yield None
        arrived(2)
        subtract(0, 1, 1, 3)
        for n, ws in enumerate(diagonal(1)):
            if n in (7, 15):
                yield None
        arrived(3)
        subtract(0, 1, 3, 4)
        eliminate(1, ws)
        subtract(0, 2, 2, 3)
        subtract(1, 2, 2, 3)
        for n, ws in enumerate(diagonal(2)):
            if n == 7:
                yield None
                arrived(4)
                arrived(5)
                for q in (2, 3):
                    subtract(0, q, 3, 4)
                    subtract(1, q, 3, 4)
        eliminate(2, ws)
        subtract(2, 3, 3, 4)
        for n, ws in enumerate(diagonal(3)):
            pass
        eliminate(3, ws)
        for p in range(NB - 2, -1, -1):
            lo, hi = 128 * p, 128 * p + 128
            for j in range(2):
                y_ref[j, :, lo:hi] = y_ref[j, :, lo:hi] - dot(y_ref[j, :, hi:], t_ref[j, p, :, hi:], 1, 1)
        for t in range(TRAITS):
            for j in range(2):
                b_ref[2 * t + j:2 * t + j + 1, :] = y_ref[j, t:t + 1, :]
        beta_ref[...] = b_ref[...].astype(jnp.bfloat16)

    solving = tasks()

    def send_relays(g):
        for c in relays(g) + plains(g):
            c.start()

    def send_combs(g):
        (zero, r0), (one, r1) = both(g)
        for c in relays(g):
            c.wait_recv()
        relay[0, r0] += part[zero + after, r0]
        relay[1, r1] += part[one + before, r1]
        for c in combs(g):
            c.start()

    def totals(g):
        (zero, r0), (one, r1) = both(g)
        for c in plains(g) + combs(g):
            c.wait_recv()
        return part[zero + y, r0] + plain[1, r0] + comb[0, r0], part[one + y, r1] + plain[0, r1] + comb[1, r1]

    def send_gathers(g):
        for k in range(FOLDS):
            @pl.when(fold_here != k)
            def _():
                gather(g, k, me).start()

            @pl.when(fold_here == k)
            def _():
                r = FOLDS * START[g] + k * ROWS[g]
                out_ref[me, START[g]:START[g] + ROWS[g], :] = done[r:r + ROWS[g], :]

    for i in range(STEPS + 3):
        if i < STEPS:
            if i in Z_FIRST:
                cross_z(i).wait_recv()
                for n in range(4):
                    part[4 * z + n, span(i)] += quarters[n, span(i)]
            else:
                products(i)
            if i == 0:
                pl.semaphore_wait(barrier, 7)
            send_relays(i)
            if 0 <= i - LEAD < len(Z_FIRST):
                products(Z_FIRST[i - LEAD])
                cross_z(Z_FIRST[i - LEAD]).start()
        if 1 <= i <= STEPS:
            send_combs(i - 1)
        if 2 <= i <= STEPS + 1:
            g = i - 2
            zero, one = totals(g)
            if g in Z_FIRST:
                n = FOLDS * ROWS[g] // 2
                done[FOLDS * START[g]:FOLDS * START[g] + n] = zero
                done[FOLDS * START[g] + n:FOLDS * START[g] + 2 * n] = one
                send_gathers(g)
            else:
                half[span(g)] = jnp.where(z == 0, one, zero)
                done[span(g)] = jnp.where(z == 0, zero, one)
                cross_z(g).start()
        if i >= 3 and i - 3 not in Z_FIRST:
            g = i - 3
            cross_z(g).wait_recv()
            done[span(g)] += zin[span(g)]
            send_gathers(g)
        if i >= FIRST:
            next(solving)

    for _ in solving:
        pass
    for g in range(STEPS):
        for c in relays(g) + plains(g) + combs(g) + [cross_z(g)]:
            c.wait_send()
        for k in range(FOLDS):
            @pl.when(fold_here != k)
            def _():
                gather(g, k, me).wait_send()


def fit(lam, x, yt, fold):
    vmem = pl.BlockSpec(memory_space=pltpu.VMEM)
    f32 = jnp.float32
    rows = FOLDS * TOTAL
    return pl.pallas_call(
        fit_kernel,
        out_shape=jax.ShapeDtypeStruct((16, BLOCK), jnp.bfloat16),
        in_specs=[pl.BlockSpec(memory_space=pltpu.SMEM), pl.BlockSpec(memory_space=pltpu.HBM), vmem, vmem],
        out_specs=vmem,
        scratch_shapes=[
            pltpu.VMEM((8, TOTAL, 128), f32),
            pltpu.VMEM((2, NB, 128, BLOCK), f32),
            pltpu.VMEM((2, NB, 128, BLOCK), f32),
            pltpu.VMEM((2, TRAITS, BLOCK), f32),
            pltpu.VMEM((16, BLOCK), f32),
            pltpu.VMEM(x.shape, jnp.bfloat16),
            pltpu.VMEM((NB, 128 * FOLDS, x.shape[0]), jnp.bfloat16),
            pltpu.VMEM((8, rows, 128), f32),
            pltpu.VMEM((2, rows, 128), f32),
            pltpu.VMEM((2, rows, 128), f32),
            pltpu.VMEM((2, rows, 128), f32),
            pltpu.VMEM((rows, 128), f32),
            pltpu.VMEM((rows, 128), f32),
            pltpu.VMEM((4, rows, 128), f32),
            pltpu.VMEM((rows, 128), f32),
            pltpu.SemaphoreType.DMA((NB,)),
            pltpu.SemaphoreType.DMA((7, STEPS)),
            pltpu.SemaphoreType.DMA((7, STEPS)),
            pltpu.SemaphoreType.DMA((STEPS, FOLDS)),
            pltpu.SemaphoreType.DMA((STEPS, 8)),
        ],
        compiler_params=pltpu.CompilerParams(collective_id=1, has_side_effects=True, vmem_limit_bytes=62 << 20),
    )(lam, x, yt, fold)


def tail_kernel(beta_ref, x_ref, fold_ref, old_ref, oof_ref, cross_ref, xv, fv, ov, betas, mine, feats, terms, rows, sums,
                load, bsend, brecv, fsend, frecv, tsend, trecv, ssend, srecv):
    s, b = lax.axis_index("smp"), lax.axis_index("blk")
    fold_here = lax.rem(3 * s, 8)
    samples = x_ref.shape[0]
    fetches = [pltpu.make_async_copy(x_ref, xv, load.at[0]), pltpu.make_async_copy(fold_ref, fv, load.at[1]),
               pltpu.make_async_copy(old_ref, ov, load.at[2])]
    for fetch in fetches:
        fetch.start()
    barrier = pltpu.get_barrier_semaphore()

    def greet_smp(i, carry):
        pl.semaphore_signal(barrier, inc=1, device_id={"smp": lax.rem(s + i, 8)}, device_id_type=MESH)
        return carry

    def greet_blk(i, carry):
        pl.semaphore_signal(barrier, inc=1, device_id={"blk": lax.rem(b + i, 16)}, device_id_type=MESH)
        return carry

    for i in range(1, 8):
        greet_smp(i, 0)
    for i in range(1, 16):
        greet_blk(i, 0)
    pl.semaphore_wait(barrier, 22)

    def spread(i):
        return pltpu.make_async_remote_copy(
            src_ref=beta_ref, dst_ref=betas.at[fold_here], send_sem=bsend.at[i], recv_sem=brecv.at[fold_here],
            device_id={"smp": lax.rem(s + i, 8)}, device_id_type=MESH)

    def start_spread(i, carry):
        spread(i).start()
        return carry

    def end_spread(i, carry):
        spread(i).wait_send()
        return carry

    @pl.when(fold_here < FOLDS)
    def _():
        for i in (5, 4, 3, 7, 1, 6, 2):
            start_spread(i, 0)
        betas[fold_here] = beta_ref[...]

    def beta_in(k, carry):
        @pl.when(fold_here != k)
        def _():
            pltpu.make_async_remote_copy(
                src_ref=beta_ref, dst_ref=betas.at[k], send_sem=bsend.at[0], recv_sem=brecv.at[k],
                device_id={"smp": lax.rem(s + 1, 8)}, device_id_type=MESH).wait_recv()
        return carry

    for fetch in fetches:
        fetch.wait()
    for k in range(FOLDS):
        beta_in(k, 0)
    flat = jnp.concatenate([betas[k] for k in range(FOLDS)], axis=0)
    fitted = lax.dot_general(flat, xv[...], (((1,), (1,)), ((), ())), preferred_element_type=jnp.float32)
    fold = fv[...]
    chosen = jnp.zeros((16, samples), jnp.float32)
    for k in range(FOLDS):
        chosen = jnp.where(fold == k, fitted[16 * k:16 * k + 16, :], chosen)
    oof = (chosen * math.sqrt(8 * samples / BLOCK)).astype(jnp.bfloat16)
    for c in range(16):
        mine[c] = oof[:, 128 * c:128 * c + 128]
    feats[b] = mine[b]

    def feature(i):
        to = lax.rem(b + i, 16)
        return pltpu.make_async_remote_copy(
            src_ref=mine.at[to], dst_ref=feats.at[b], send_sem=fsend.at[i], recv_sem=frecv.at[i],
            device_id={"blk": to}, device_id_type=MESH)

    def start_feature(i, carry):
        feature(i).start()
        return carry

    def end_feature(i, carry):
        feature(i).wait_recv()
        return carry

    for i in range(1, 16):
        start_feature(i, 0)
    oof_ref[...] = oof
    r = lax.broadcasted_iota(jnp.int32, (256, 512), 0)
    c = lax.broadcasted_iota(jnp.int32, (256, 512), 1)
    same = ((r >> 1) & 7) == jnp.where(c < 256, c >> 5, (c >> 1) & 7)
    r = lax.broadcasted_iota(jnp.int32, (512, 128), 0)
    c = lax.broadcasted_iota(jnp.int32, (512, 128), 1)
    place = jnp.where(r < 256, r & 31, 32 + (((r - 256) >> 4) << 1) + (r & 1))
    pick = jnp.where(place == c, 1.0, 0.0).astype(jnp.bfloat16)
    for i in range(1, 16):
        end_feature(i, 0)
    f = jnp.concatenate([feats[c] for c in range(16)], axis=0)
    nt = (((1,), (1,)), ((), ()))
    against = lax.dot_general(f, jnp.concatenate([ov[...], f], axis=0), nt, preferred_element_type=jnp.float32)
    chosen = jnp.where(same, against, 0.0)
    hi = chosen.astype(jnp.bfloat16)
    rest = chosen - hi.astype(jnp.float32)
    mid = rest.astype(jnp.bfloat16)
    low = (rest - mid.astype(jnp.float32)).astype(jnp.bfloat16)
    total = jnp.dot(hi, pick, preferred_element_type=jnp.float32)
    total += jnp.dot(mid, pick, preferred_element_type=jnp.float32)
    total += jnp.dot(low, pick, preferred_element_type=jnp.float32)
    for k in range(16):
        terms[k] = total[16 * k:16 * k + 16, :]
    rows[b] = terms[b]

    def term(i):
        to = lax.rem(b + i, 16)
        return pltpu.make_async_remote_copy(
            src_ref=terms.at[to], dst_ref=rows.at[b], send_sem=tsend.at[i], recv_sem=trecv.at[i],
            device_id={"blk": to}, device_id_type=MESH)

    def start_term(i, carry):
        term(i).start()
        return carry

    def end_term(i, carry):
        term(i).wait_recv()
        return carry

    for i in range(1, 16):
        start_term(i, 0)
    for i in range(1, 16):
        end_term(i, 0)
    part = rows[0]
    for k in range(1, 16):
        part = part + rows[k]
    sums[s] = part

    def last(i):
        return pltpu.make_async_remote_copy(
            src_ref=sums.at[s], dst_ref=sums.at[s], send_sem=ssend.at[i], recv_sem=srecv.at[i],
            device_id={"smp": lax.rem(s + i, 8)}, device_id_type=MESH)

    def start_last(i, carry):
        last(i).start()
        return carry

    def end_last(i, carry):
        last(i).wait_recv()
        return carry

    for i in (5, 4, 3, 7, 1, 6, 2):
        start_last(i, 0)
    for i in range(1, 8):
        end_last(i, 0)
    final = sums[0]
    for k in range(1, 8):
        final = final + sums[k]
    cross_ref[...] = final * (1.0 / (8 * samples))
    for i in range(1, 16):
        feature(i).wait_send()
        term(i).wait_send()
    for i in range(1, 8):
        last(i).wait_send()

    @pl.when(fold_here < FOLDS)
    def _():
        for i in range(1, 8):
            end_spread(i, 0)


def tail(beta, x, fold, old):
    vmem = pl.BlockSpec(memory_space=pltpu.VMEM)
    dma = pltpu.SemaphoreType.DMA
    return pl.pallas_call(
        tail_kernel,
        out_shape=(jax.ShapeDtypeStruct((16, x.shape[0]), jnp.bfloat16), jax.ShapeDtypeStruct((16, 128), jnp.float32)),
        in_specs=[vmem] + [pl.BlockSpec(memory_space=pltpu.HBM)] * 3,
        out_specs=(vmem, vmem),
        scratch_shapes=[
            pltpu.VMEM(x.shape, jnp.bfloat16),
            pltpu.VMEM(fold.shape, jnp.int32),
            pltpu.VMEM(old.shape, jnp.bfloat16),
            pltpu.VMEM((FOLDS, 16, BLOCK), jnp.bfloat16),
            pltpu.VMEM((16, 16, 128), jnp.bfloat16),
            pltpu.VMEM((16, 16, 128), jnp.bfloat16),
            pltpu.VMEM((16, 16, 128), jnp.float32),
            pltpu.VMEM((16, 16, 128), jnp.float32),
            pltpu.VMEM((8, 16, 128), jnp.float32),
            dma((3,)), dma((8,)), dma((8,)), dma((16,)), dma((16,)), dma((16,)), dma((16,)), dma((8,)), dma((8,)),
        ],
        compiler_params=pltpu.CompilerParams(collective_id=2, has_side_effects=True, vmem_limit_bytes=62 << 20),
    )(beta, x, fold, old)


def local(x, y, fold, lam, old):
    rows = x.shape[0]
    fold = fold[None, :]
    beta = fit(lam, x, y.T, fold)
    before = jnp.transpose(old[0], (1, 2, 0)).reshape(256, 128)
    oof, cross = tail(beta, x, fold, before)
    here = lax.dynamic_slice_in_dim(cross, 8 * lax.axis_index("smp"), 8, 1)
    return jnp.transpose(oof.reshape(TRAITS, 2, rows), (2, 0, 1)), here.reshape(TRAITS, 2, 8)


def solution(mesh):
    return jax.shard_map(
        local,
        mesh=mesh,
        in_specs=(P("smp", "blk"), P("smp", None), P("smp"), P(), P("smp", "blk", None, None)),
        out_specs=(P("smp", None, "blk"), P(None, "blk", "smp")),
        check_vma=False,
    )
```
